32 devices in a mesh: groups: 2 (over x), space: 16 (over z, y, core).
Axes of the slice: x: 2, y: 2, z: 4, core: 2. Of those that a mesh axis runs over, the one named last changes fastest.
Arguments:
- signal: float32 [65536, 128], P(('groups', 'space')), parts along dimension 0, may hold values from -12 to 12
- space_tiles: float32 [512, 64, 384], P('space'), may hold values from -0.3125 to 0.3125
- tree_precision: float32 [256, 128], P('groups'), parts along dimension 0, may hold values from -0.5 to 0.5
- send_tiles: int32 [16, 4, 8], P('space'), may hold values from 0 to 31, as said below
- column_tiles: int32 [512, 6], P('space'), may hold values from 0 to 63, as said below
Outputs:
- product: float32 [65536, 128], P(('groups', 'space')), parts along dimension 0
- quad_form: float32 [2], P('groups'), parts along dimension 0
The draws below stay inside these ranges and needn't reach their ends.
There are 2 independent parts, one for each index of `groups`. The reference program is written for one: setup_inputs(seed, part) draws one part's arguments, and reference() takes and returns one part's arrays. A program takes and returns all parts, laid end to end along the dimension named above; an argument that names none is the same for every part. Nothing has to cross between parts.
Inputs may be any that keep to these rules, and one draw needn't show every extreme that they name: `send_tiles`: within one list the tile numbers are distinct; a partition lists tiles only towards neighbours that exist on the grid, from 1 to 8 of them, and some partition lists 8 tiles east and another south; slots past a list's length hold other tiles. `column_tiles`: entry 0 of every tile row is the row's own tile; entries below 32 are the partition's own tiles; an entry 32 + d * 8 + j names slot j of the list received from direction d, and only slots within that list's length.
All inputs are finite; a program needn't handle non-finite values.
Results may differ from the reference program's by a relative error of at most 0.00022.
Values sent between devices are 32-bit elements; how exact they have to be, the bound alone decides.
A program may use at most 64 MiB of HBM per device.

```python
import math
import jax
import jax.numpy as jnp
from jax import lax

S = 128
TN = 64
TD = 32
K = 6
CAP = 8
NODES = 32768
NODE_TILES = 512
N_SPACE = 16


def layout_draw(key):
    wide = N_SPACE // 8
    device = jnp.arange(N_SPACE, dtype=jnp.int32)
    column = device % wide
    rowpos = device // wide
    exists = jnp.stack([column < wide - 1, column > 0, rowpos < 7, rowpos > 0], axis=1)
    counts = jax.random.randint(jax.random.fold_in(key, 11), (N_SPACE, 4), 1, CAP + 1)
    counts = counts.at[0, 0].set(CAP).at[wide, 3].set(CAP)
    counts = jnp.where(exists, counts, 0).astype(jnp.int32)
    scores = jax.random.randint(jax.random.fold_in(key, 12), (N_SPACE, 4, TD), 0, 1 << 20)
    scores = scores * TD + jnp.arange(TD, dtype=jnp.int32)
    order = jnp.argsort(scores, axis=-1)[..., :CAP].astype(jnp.int32)
    return (counts, order)


def draw_send_tiles(key, part):
    counts, order = layout_draw(key)
    return order


def draw_column_tiles(key, part):
    counts, order = layout_draw(key)
    wide = N_SPACE // 8
    device = jnp.arange(N_SPACE, dtype=jnp.int32)
    steps = jnp.array([1, -1, wide, -wide], dtype=jnp.int32)
    sender = (device[:, None] - steps[None, :]) % N_SPACE
    received = counts[sender, jnp.arange(4, dtype=jnp.int32)[None, :]]
    rowtile = jnp.arange(TD, dtype=jnp.int32)
    local_pick = jax.random.randint(jax.random.fold_in(key, 13), (N_SPACE, TD, 5), 0, TD).astype(jnp.int32)
    entries = [jnp.broadcast_to(rowtile[None, :], (N_SPACE, TD))]
    for direction in range(4):
        remote = rowtile[None, :] < received[:, direction][:, None]
        slot_index = TD + direction * CAP + rowtile[None, :]
        entries.append(jnp.where(remote, slot_index, local_pick[:, :, direction]))
    entries.append(local_pick[:, :, 4])
    return jnp.stack(entries, axis=2).reshape(N_SPACE * TD, K).astype(jnp.int32)


def draw_signal(key, part):
    rows = jnp.arange(NODES, dtype=jnp.float32)[:, None]
    rise = 3.0 ** (0.5 * rows / NODES)
    species = jnp.exp(jax.random.uniform(jax.random.fold_in(key, 21), (1, S), jnp.float32, 0.0, math.log(3.2)))
    base = jax.random.normal(jax.random.fold_in(key, 23), (NODES, S), jnp.float32)
    values = base * rise * species
    return jnp.clip(values, -12.0, 12.0).astype(jnp.float32)


def block_scale(own_key, shape, split, smallest, top_value):
    def one(position, shards_of):
        draws = jax.random.uniform(jax.random.fold_in(jax.random.fold_in(own_key, 6), position), (shards_of,), jnp.float32, smallest / len(split), top_value / len(split))
        return jnp.repeat(jnp.exp(draws), shape[position] // shards_of).reshape((-1,) + (1,) * (len(shape) - position - 1))

    gain = one(*split[0])
    for cut in split[1:]:
        gain = gain * one(*cut)
    return gain


def noise(stream_key, extent, width, bound, cuts=(), kind=jnp.bfloat16):
    values = width * jax.random.normal(stream_key, extent, jnp.float32)
    if cuts:
        values = values * block_scale(stream_key, extent, cuts, -0.22, 0.18)
    return jnp.clip(values, -bound, bound).astype(kind)


def setup_inputs(seed: int = 0, part: int = 0) -> dict:
    key_list = jax.random.split(jax.random.key(seed), 6)
    own_keys = jax.random.split(jax.random.fold_in(key_list[5], part), 6)
    return {
        "signal": draw_signal(jax.random.fold_in(jax.random.fold_in(key_list[5], part), 71), part),
        "space_tiles": noise(key_list[1], (NODE_TILES, TN, K * TN), (K * TN) ** -0.5, 0.3125, ((0, 16),), jnp.float32),
        "tree_precision": noise(own_keys[2], (S, S), S ** -0.5, 0.5, (), jnp.float32),
        "send_tiles": draw_send_tiles(jax.random.fold_in(key_list[5], 71), part),
        "column_tiles": draw_column_tiles(jax.random.fold_in(key_list[5], 71), part),
    }


def global_columns(send_tiles, column_tiles):
    wide = N_SPACE // 8
    steps = jnp.array([1, -1, wide, -wide], dtype=jnp.int32)
    owner = (jnp.arange(NODE_TILES, dtype=jnp.int32) // TD)[:, None]
    local_part = jnp.minimum(column_tiles, TD - 1)
    remote = jnp.maximum(column_tiles - TD, 0)
    direction = remote // CAP
    slot = remote % CAP
    sender = (owner - steps[direction]) % N_SPACE
    listed = send_tiles[sender, direction, slot]
    return jnp.where(column_tiles < TD, owner * TD + local_part, sender * TD + listed).astype(jnp.int32)

def reference(signal, space_tiles, tree_precision, send_tiles, column_tiles):
    columns = global_columns(send_tiles, column_tiles)
    tiled = signal.reshape(NODE_TILES, TN, S)
    col_blocks = columns.reshape(N_SPACE, TD, K)
    tile_blocks = space_tiles.reshape(N_SPACE, TD, TN, K * TN)

    def one_part(pair):
        cols, tiles = pair
        gathered = tiled[cols].reshape(TD, K * TN, S)
        return jnp.einsum('rac,rcs->ras', tiles, gathered, precision=lax.Precision.HIGHEST)
    spatial = lax.map(one_part, (col_blocks, tile_blocks)).reshape(NODES, S)
    product = jnp.dot(spatial, tree_precision.T, precision=lax.Precision.HIGHEST, preferred_element_type=jnp.float32)
    quad_form = jnp.sum(signal * product) / jnp.sqrt(jnp.float32(NODES * S))
    return (product, quad_form.reshape(1))
```

```python
import functools
import math

import jax
import jax.numpy as jnp
from jax import lax
from jax.experimental import pallas as pl
from jax.experimental.pallas import tpu as pltpu
from jax.sharding import PartitionSpec as P

ROWS = 8
CHUNKS = 4
MESH = pl.DeviceIdType.MESH


def halves(value):
    high = value.astype(jnp.bfloat16)
    low = (value - high.astype(jnp.float32)).astype(jnp.bfloat16)
    return high, low


def kernel(
    count, scaling,
    signal_ref, tiles_ref, tree_ref, send_ref, column_ref,
    product_ref, quad_ref,
    x, tiles, a, xs, z, spatial, outgoing, received, out, shares,
    x_sem, tiles_sem, send_sem, recv_sem, share_send, share_recv, out_sem,
):
    tile_rows, nodes, species = x.shape
    stored = column_ref.shape[1]
    capacity = send_ref.shape[1]
    wide = count // ROWS
    me = lax.axis_index("space")
    column, row = lax.rem(me, wide), me // wide
    not_first, not_last = column > 0, column < wide - 1
    above, below = row > 0, row < ROWS - 1
    sends = (not_last, not_first, below, above)
    receives = (not_first, not_last, above, below)
    targets = (me + 1, me - 1, me + wide, me - wide)

    load_x = pltpu.make_async_copy(signal_ref, x, x_sem)
    load_x.start()
    part = tile_rows // CHUNKS
    loads = []
    for c in range(CHUNKS):
        piece = pl.ds(c * part, part)
        loads.append(pltpu.make_async_copy(tiles_ref.at[piece], tiles.at[piece], tiles_sem.at[c]))
        loads[-1].start()

    barrier = pltpu.get_barrier_semaphore()

    def greet(i, carry):
        pl.semaphore_signal(
            barrier, inc=1, device_id={"space": lax.rem(me + i, count)}, device_id_type=MESH
        )
        return carry

    lax.fori_loop(1, count, greet, 0)

    load_x.wait()

    def copy_for(d):
        return pltpu.make_async_remote_copy(
            src_ref=outgoing.at[d],
            dst_ref=received.at[d],
            send_sem=send_sem.at[d],
            recv_sem=recv_sem.at[d],
            device_id={"space": targets[d]},
            device_id_type=MESH,
        )

    for d in (2, 3, 0, 1):
        for j in range(capacity):
            outgoing[d, j] = x[send_ref[d, j]]
    pl.semaphore_wait(barrier, count - 1)
    for d in (2, 3, 0, 1):
        @pl.when(sends[d])
        def _():
            copy_for(d).start()

    tree = tree_ref[...]
    zero = jnp.zeros((species, species), jnp.bfloat16)

    def doubled(matrix):
        high, low = halves(matrix)
        return jnp.concatenate(
            [jnp.concatenate([high, low], 1), jnp.concatenate([high, zero], 1)], 0
        )

    def times(paired, weights):
        both = jnp.dot(paired, weights, preferred_element_type=jnp.float32)
        return both[:, :species] + both[:, species:]

    right, right_t = doubled(tree), doubled(tree.T)

    def prepare(t, carry):
        high, low = halves(x[t])
        paired = jnp.concatenate([high, low], 1)
        xs[t] = paired
        z[t] = times(paired, right)
        return carry

    lax.fori_loop(0, tile_rows, prepare, 0)
    for load in loads:
        load.wait()

    def cut(t, carry):
        high, low = halves(tiles[t])
        a[t] = jnp.concatenate([high, low], 0)
        return carry

    lax.fori_loop(0, tile_rows, cut, 0)

    for d in (0, 1, 2, 3):
        @pl.when(receives[d])
        def _():
            copy_for(d).wait_recv()
            for j in range(capacity):
                high, low = halves(received[d, j])
                xs[tile_rows + d * capacity + j] = jnp.concatenate([high, low], 1)

    def multiply(t, acc):
        block = jnp.concatenate([xs[column_ref[t, k]] for k in range(stored)], 0)
        both = jnp.dot(a[t], block, preferred_element_type=jnp.float32)
        small = both[:nodes, species:] + both[nodes:, :species] + both[nodes:, species:]
        result = both[:nodes, :species] + small
        spatial[t] = result
        return acc + jnp.sum((z[t] * result).reshape(nodes // 8, 8, species), axis=0)

    acc = lax.fori_loop(
        0, tile_rows, multiply, jnp.zeros((8, species), jnp.float32), unroll=4
    )

    shares[me] = acc

    def share_copy(i):
        return pltpu.make_async_remote_copy(
            src_ref=shares.at[me],
            dst_ref=shares.at[me],
            send_sem=share_send.at[i],
            recv_sem=share_recv.at[i],
            device_id={"space": lax.rem(me + i, count)},
            device_id_type=MESH,
        )

    def give(i, carry):
        share_copy(i).start()
        return carry

    lax.fori_loop(1, count, give, 0)

    stores = []
    for c in range(CHUNKS):
        piece = pl.ds(c * part, part)
        high, low = halves(spatial[piece].reshape(part * nodes, species))
        result = times(jnp.concatenate([high, low], 1), right_t)
        out[piece] = result.reshape(part, nodes, species)
        stores.append(pltpu.make_async_copy(out.at[piece], product_ref.at[piece], out_sem.at[c]))
        stores[-1].start()

    for d in range(4):
        @pl.when(sends[d])
        def _():
            copy_for(d).wait_send()

    def take(i, carry):
        share_copy(i).wait_recv()
        return carry

    lax.fori_loop(1, count, take, 0)

    def sent(i, carry):
        share_copy(i).wait_send()
        return carry

    lax.fori_loop(1, count, sent, 0)
    quad_ref[0] = jnp.sum(jnp.sum(shares[...], axis=0)) * scaling
    for store in stores:
        store.wait()


def on_device(signal, space_tiles, tree_precision, send_tiles, column_tiles):
    count = lax.axis_size("space")
    tile_rows, nodes, width = space_tiles.shape
    species = signal.shape[1]
    directions, capacity = send_tiles.shape[1:]
    scaling = 1.0 / math.sqrt(count * tile_rows * nodes * species)
    vmem, f32, bf16 = pltpu.VMEM, jnp.float32, jnp.bfloat16
    dma = pltpu.SemaphoreType.DMA
    everywhere = pl.BlockSpec(memory_space=pl.ANY)
    smem = pl.BlockSpec(memory_space=pltpu.SMEM)
    field = (tile_rows, nodes, species)
    lists = (directions, capacity, nodes, species)
    product, quad = pl.pallas_call(
        functools.partial(kernel, count, scaling),
        out_shape=(jax.ShapeDtypeStruct(field, f32), jax.ShapeDtypeStruct((1,), f32)),
        in_specs=[everywhere, everywhere, pl.BlockSpec(memory_space=vmem), smem, smem],
        out_specs=(everywhere, smem),
        scratch_shapes=[
            vmem(field, f32),
            vmem(space_tiles.shape, f32),
            vmem((tile_rows, 2 * nodes, width), bf16),
            vmem((tile_rows + directions * capacity, nodes, 2 * species), bf16),
            vmem(field, f32),
            vmem(field, f32),
            vmem(lists, f32),
            vmem(lists, f32),
            vmem(field, f32),
            vmem((count, 8, species), f32),
            dma,
            dma((CHUNKS,)),
            dma((directions,)),
            dma((directions,)),
            dma((count,)),
            dma((count,)),
            dma((CHUNKS,)),
        ],
        compiler_params=pltpu.CompilerParams(
            collective_id=0, has_side_effects=True, vmem_limit_bytes=40 * 2**20
        ),
        cost_estimate=pl.CostEstimate(
            flops=2 * tile_rows * nodes * species * (width + 2 * species),
            bytes_accessed=4 * (space_tiles.size + 2 * signal.size),
            transcendentals=0,
        ),
        name="kronecker_product",
    )(signal.reshape(field), space_tiles, tree_precision, send_tiles[0], column_tiles)
    return product.reshape(signal.shape), quad


def solution(mesh):
    placed = (
        P(("groups", "space"), None),
        P("space", None, None),
        P("groups", None),
        P("space", None, None),
        P("space", None),
    )
    return jax.shard_map(
        on_device,
        mesh=mesh,
        in_specs=placed,
        out_specs=(P(("groups", "space"), None), P("groups")),
        check_vma=False,
    )
```

```python
import functools
import math

import jax
import jax.numpy as jnp
from jax import lax
from jax.experimental import pallas as pl
from jax.experimental.pallas import tpu as pltpu
from jax.sharding import PartitionSpec as P

ROWS = 8
CHUNKS = 4
MESH = pl.DeviceIdType.MESH


def halves(value):
    high = value.astype(jnp.bfloat16)
    low = (value - high.astype(jnp.float32)).astype(jnp.bfloat16)
    return high, low


def kernel(
    count, scaling,
    signal_ref, tiles_ref, tree_ref, send_ref, column_ref,
    product_ref, quad_ref,
    x, tiles, tree_in, send_in, column_in, a, xs, z, spatial, outgoing, received, shares,
    x_sem, small_sem, tiles_sem, send_sem, recv_sem, share_send, share_recv,
):
    tile_rows, nodes, species = x.shape
    stored = column_ref.shape[0]
    capacity = send_ref.shape[1]
    load_send = pltpu.make_async_copy(send_ref, send_in, small_sem.at[0])
    load_send.start()
    load_x = pltpu.make_async_copy(signal_ref, x, x_sem)
    load_x.start()
    load_tree = pltpu.make_async_copy(tree_ref, tree_in, small_sem.at[1])
    load_tree.start()
    load_column = pltpu.make_async_copy(column_ref, column_in, small_sem.at[2])
    load_column.start()
    wide = count // ROWS
    me = lax.axis_index("space")
    column, row = lax.rem(me, wide), me // wide
    not_first, not_last = column > 0, column < wide - 1
    above, below = row > 0, row < ROWS - 1
    sends = (not_last, not_first, below, above)
    receives = (not_first, not_last, above, below)
    targets = (me + 1, me - 1, me + wide, me - wide)

    part = tile_rows // CHUNKS
    loads = []
    for c in range(CHUNKS):
        piece = pl.ds(c * part, part)
        loads.append(pltpu.make_async_copy(tiles_ref.at[piece], tiles.at[piece], tiles_sem.at[c]))
        loads[-1].start()

    barrier = pltpu.get_barrier_semaphore()

    def greet(i, carry):
        pl.semaphore_signal(
            barrier, inc=1, device_id={"space": lax.rem(me + i, count)}, device_id_type=MESH
        )
        return carry

    lax.fori_loop(1, count, greet, 0)

    load_send.wait()
    load_x.wait()

    def copy_for(d):
        return pltpu.make_async_remote_copy(
            src_ref=outgoing.at[d],
            dst_ref=received.at[d],
            send_sem=send_sem.at[d],
            recv_sem=recv_sem.at[d],
            device_id={"space": targets[d]},
            device_id_type=MESH,
        )

    for d in (2, 3, 0, 1):
        for j in range(capacity):
            outgoing[d, j] = x[send_in[d, j]]
        if d == 2:
            pl.semaphore_wait(barrier, count - 1)

        @pl.when(sends[d])
        def _():
            copy_for(d).start()

    load_tree.wait()
    tree = tree_in[...]
    zero = jnp.zeros((species, species), jnp.bfloat16)

    def doubled(matrix):
        high, low = halves(matrix)
        return jnp.concatenate(
            [jnp.concatenate([high, low], 1), jnp.concatenate([high, zero], 1)], 0
        )

    def times(paired, weights):
        both = jnp.dot(paired, weights, preferred_element_type=jnp.float32)
        return both[:, :species] + both[:, species:]

    right, right_t = doubled(tree), doubled(tree.T)

    def prepare(c, carry):
        piece = pl.ds(c * part, part)
        high, low = halves(x[piece])
        paired = jnp.concatenate([high, low], 2)
        xs[piece] = paired
        result = times(paired.reshape(part * nodes, 2 * species), right)
        z[piece] = result.reshape(part, nodes, species)
        return carry

    lax.fori_loop(0, CHUNKS, prepare, 0)
    for load in loads:
        load.wait()

    def cut(t, carry):
        high, low = halves(tiles[t])
        a[t] = jnp.concatenate([high, low], 0)
        return carry

    lax.fori_loop(0, tile_rows, cut, 0, unroll=4)
    load_column.wait()

    for d in (0, 1, 2, 3):
        @pl.when(receives[d])
        def _():
            copy_for(d).wait_recv()
            for j in range(capacity):
                high, low = halves(received[d, j])
                xs[tile_rows + d * capacity + j] = jnp.concatenate([high, low], 1)

    def multiply(t, acc):
        block = jnp.concatenate([xs[column_in[k, t]] for k in range(stored)], 0)
        both = jnp.dot(a[t], block, preferred_element_type=jnp.float32)
        small = both[:nodes, species:] + both[nodes:, :species] + both[nodes:, species:]
        result = both[:nodes, :species] + small
        spatial[t] = result
        return acc + jnp.sum((z[t] * result).reshape(nodes // 8, 8, species), axis=0)

    acc = lax.fori_loop(
        0, tile_rows, multiply, jnp.zeros((8, species), jnp.float32), unroll=8
    )

    shares[me] = acc

    def share_copy(i):
        return pltpu.make_async_remote_copy(
            src_ref=shares.at[me],
            dst_ref=shares.at[me],
            send_sem=share_send.at[i],
            recv_sem=share_recv.at[i],
            device_id={"space": lax.rem(me + i, count)},
            device_id_type=MESH,
        )

    def give(i, carry):
        share_copy(i).start()
        return carry

    lax.fori_loop(1, count, give, 0)

    for c in range(CHUNKS):
        piece = pl.ds(c * part, part)
        high, low = halves(spatial[piece].reshape(part * nodes, species))
        result = times(jnp.concatenate([high, low], 1), right_t)
        product_ref[piece] = result.reshape(part, nodes, species)

    for d in range(4):
        @pl.when(sends[d])
        def _():
            copy_for(d).wait_send()

    def take(i, carry):
        share_copy(i).wait_recv()
        return carry

    lax.fori_loop(1, count, take, 0)

    def sent(i, carry):
        share_copy(i).wait_send()
        return carry

    lax.fori_loop(1, count, sent, 0)
    quad_ref[0] = jnp.sum(jnp.sum(shares[...], axis=0)) * scaling


def on_device(signal, space_tiles, tree_precision, send_tiles, column_tiles):
    count = lax.axis_size("space")
    tile_rows, nodes, width = space_tiles.shape
    species = signal.shape[1]
    directions, capacity = send_tiles.shape[1:]
    scaling = 1.0 / math.sqrt(count * tile_rows * nodes * species)
    vmem, f32, bf16 = pltpu.VMEM, jnp.float32, jnp.bfloat16
    dma = pltpu.SemaphoreType.DMA
    hbm = pl.BlockSpec(memory_space=pltpu.HBM)
    smem = pl.BlockSpec(memory_space=pltpu.SMEM)
    field = (tile_rows, nodes, species)
    lists = (directions, capacity, nodes, species)
    product, quad = pl.pallas_call(
        functools.partial(kernel, count, scaling),
        out_shape=(pltpu.VMEM(field, f32), jax.ShapeDtypeStruct((1,), f32)),
        in_specs=[hbm] * 5,
        out_specs=(pl.BlockSpec(memory_space=vmem), smem),
        scratch_shapes=[
            vmem(field, f32),
            vmem(space_tiles.shape, f32),
            vmem(tree_precision.shape, f32),
            pltpu.SMEM((directions, capacity), jnp.int32),
            pltpu.SMEM(column_tiles.shape[::-1], jnp.int32),
            vmem((tile_rows, 2 * nodes, width), bf16),
            vmem((tile_rows + directions * capacity, nodes, 2 * species), bf16),
            vmem(field, f32),
            vmem(field, f32),
            vmem(lists, f32),
            vmem(lists, f32),
            vmem((count, 8, species), f32),
            dma,
            dma((3,)),
            dma((CHUNKS,)),
            dma((directions,)),
            dma((directions,)),
            dma((count,)),
            dma((count,)),
        ],
        compiler_params=pltpu.CompilerParams(
            collective_id=0, has_side_effects=True, vmem_limit_bytes=40 * 2**20
        ),
        cost_estimate=pl.CostEstimate(
            flops=2 * tile_rows * nodes * species * (width + 2 * species),
            bytes_accessed=4 * (space_tiles.size + 2 * signal.size),
            transcendentals=0,
        ),
        name="kronecker_product",
    )(*(
        pltpu.with_memory_space_constraint(array, pltpu.HBM)
        for array in (signal.reshape(field), space_tiles, tree_precision, send_tiles[0], column_tiles.T)
    ))
    return product.reshape(signal.shape), quad


def solution(mesh):
    placed = (
        P(("groups", "space"), None),
        P("space", None, None),
        P("groups", None),
        P("space", None, None),
        P("space", None),
    )
    return jax.shard_map(
        on_device,
        mesh=mesh,
        in_specs=placed,
        out_specs=(P(("groups", "space"), None), P("groups")),
        check_vma=False,
    )
```

```python
import functools
import math

import jax
import jax.numpy as jnp
from jax import lax
from jax.experimental import pallas as pl
from jax.experimental.pallas import tpu as pltpu
from jax.sharding import PartitionSpec as P

ROWS = 8
CHUNKS = 4
MESH = pl.DeviceIdType.MESH


def halves(value):
    high = value.astype(jnp.bfloat16)
    low = (value - high.astype(jnp.float32)).astype(jnp.bfloat16)
    return high, low


def kernel(
    count, scaling,
    signal_ref, tiles_ref, tree_ref, send_ref, column_ref,
    product_ref, quad_ref,
    x, tiles, tree_in, send_in, column_in, a, xs, extended, pull, outgoing, received,
    inner_shares, outer_shares,
    x_sem, small_sem, tiles_sem, send_sem, recv_sem, inner_send, inner_recv, outer_send, outer_recv,
):
    tile_rows, nodes, species = x.shape
    stored = column_ref.shape[0]
    capacity = send_ref.shape[1]
    load_send = pltpu.make_async_copy(send_ref, send_in, small_sem.at[0])
    load_send.start()
    load_x = pltpu.make_async_copy(signal_ref, x, x_sem)
    load_x.start()
    load_tree = pltpu.make_async_copy(tree_ref, tree_in, small_sem.at[1])
    load_tree.start()
    load_column = pltpu.make_async_copy(column_ref, column_in, small_sem.at[2])
    load_column.start()
    wide = count // ROWS
    me = lax.axis_index("space")
    column, row = lax.rem(me, wide), me // wide
    not_first, not_last = column > 0, column < wide - 1
    above, below = row > 0, row < ROWS - 1
    sends = (not_last, not_first, below, above)
    receives = (not_first, not_last, above, below)
    targets = (me + 1, me - 1, me + wide, me - wide)

    part = tile_rows // CHUNKS
    loads = []
    for c in range(CHUNKS):
        piece = pl.ds(c * part, part)
        loads.append(pltpu.make_async_copy(tiles_ref.at[piece], tiles.at[piece], tiles_sem.at[c]))
        loads[-1].start()

    inner, outer = inner_shares.shape[0], outer_shares.shape[0]
    spot, team = lax.rem(me, inner), me // inner
    mates = [team * inner + lax.rem(spot + i, inner) for i in range(1, inner)]
    peers = [spot + inner * lax.rem(team + i, outer) for i in range(1, outer)]

    barrier = pltpu.get_barrier_semaphore()

    def greet(device):
        pl.semaphore_signal(barrier, inc=1, device_id={"space": device}, device_id_type=MESH)

    for d in range(4):
        pl.when(sends[d])(functools.partial(greet, targets[d]))
    for device in mates + peers:
        greet(device)
    greeted = len(mates) + len(peers) + sum(jnp.where(has, 1, 0) for has in receives)

    load_send.wait()
    load_x.wait()

    def copy_for(d):
        return pltpu.make_async_remote_copy(
            src_ref=outgoing.at[d],
            dst_ref=received.at[d],
            send_sem=send_sem.at[d],
            recv_sem=recv_sem.at[d],
            device_id={"space": targets[d]},
            device_id_type=MESH,
        )

    for d in (2, 3, 0, 1):
        for j in range(capacity):
            outgoing[d, j] = x[send_in[d, j]]
        if d == 2:
            pl.semaphore_wait(barrier, greeted)

        @pl.when(sends[d])
        def _():
            copy_for(d).start()

    load_tree.wait()
    tree = tree_in[...]
    zero = jnp.zeros((species, species), jnp.bfloat16)

    def doubled(matrix):
        high, low = halves(matrix)
        return jnp.concatenate(
            [jnp.concatenate([high, low], 1), jnp.concatenate([high, zero], 1)], 0
        )

    def times(paired, weights):
        both = jnp.dot(paired, weights, preferred_element_type=jnp.float32)
        return both[:, :species] + both[:, species:]

    right, right_t = doubled(tree), doubled(tree.T)

    for load in loads:
        load.wait()

    def prepare(c, carry):
        piece = pl.ds(c * part, part)
        own = x[piece]
        extended[piece] = own
        high, low = halves(own)
        paired = jnp.concatenate([high, low], 2)
        xs[piece] = paired
        weighted = times(paired.reshape(part * nodes, 2 * species), right)
        weighted = weighted.reshape(part, nodes, species)
        for i in range(part):
            t = c * part + i
            high, low = halves(tiles[t])
            stacked = jnp.concatenate([high, low], 0)
            a[t] = stacked
            high, low = halves(weighted[i])
            high_low = jnp.concatenate([high, low], 1)
            both = lax.dot_general(
                stacked,
                jnp.concatenate([high_low, high_low], 0),
                (((0,), (0,)), ((), ())),
                preferred_element_type=jnp.float32,
            )
            pull[t] = (both[:, :species] + both[:, species:]).reshape(stored, nodes, species)
        return carry

    lax.fori_loop(0, CHUNKS, prepare, 0)
    load_column.wait()

    for d in (0, 1, 2, 3):
        @pl.when(receives[d])
        def _():
            copy_for(d).wait_recv()
            for j in range(capacity):
                tile = received[d, j]
                extended[tile_rows + d * capacity + j] = tile
                high, low = halves(tile)
                xs[tile_rows + d * capacity + j] = jnp.concatenate([high, low], 1)

    def weigh(t, acc):
        for k in range(stored):
            term = pull[t, k] * extended[column_in[k, t]]
            acc = acc + jnp.sum(term.reshape(nodes // 8, 8, species), axis=0)
        return acc

    inner_shares[spot] = lax.fori_loop(
        0, tile_rows, weigh, jnp.zeros((8, species), jnp.float32), unroll=4
    )

    def share_copies(shares, mine, send, receive, devices):
        return [
            pltpu.make_async_remote_copy(
                src_ref=shares.at[mine],
                dst_ref=shares.at[mine],
                send_sem=send.at[i],
                recv_sem=receive.at[i],
                device_id={"space": device},
                device_id_type=MESH,
            )
            for i, device in enumerate(devices)
        ]

    first = share_copies(inner_shares, spot, inner_send, inner_recv, mates)
    second = share_copies(outer_shares, team, outer_send, outer_recv, peers)
    for copy in first:
        copy.start()

    for c in range(CHUNKS):
        if c == CHUNKS // 2:
            for copy in first:
                copy.wait_recv()
            outer_shares[team] = jnp.sum(inner_shares[...], axis=0)
            for copy in second:
                copy.start()
        rows = []
        for t in range(c * part, (c + 1) * part):
            block = jnp.concatenate([xs[column_in[k, t]] for k in range(stored)], 0)
            both = jnp.dot(a[t], block, preferred_element_type=jnp.float32)
            small = both[:nodes, species:] + both[nodes:, :species] + both[nodes:, species:]
            rows.append(both[:nodes, :species] + small)
        high, low = halves(jnp.concatenate(rows, 0))
        result = times(jnp.concatenate([high, low], 1), right_t)
        product_ref[pl.ds(c * part, part)] = result.reshape(part, nodes, species)

    for d in range(4):
        @pl.when(sends[d])
        def _():
            copy_for(d).wait_send()
    for copy in second:
        copy.wait_recv()
    quad_ref[0] = jnp.sum(jnp.sum(outer_shares[...], axis=0)) * scaling
    for copy in first + second:
        copy.wait_send()


def on_device(signal, space_tiles, tree_precision, send_tiles, column_tiles):
    count = lax.axis_size("space")
    tile_rows, nodes, width = space_tiles.shape
    species = signal.shape[1]
    directions, capacity = send_tiles.shape[1:]
    stored = column_tiles.shape[1]
    inner = max(i for i in range(1, math.isqrt(count) + 1) if count % i == 0)
    scaling = 1.0 / math.sqrt(count * tile_rows * nodes * species)
    vmem, f32, bf16 = pltpu.VMEM, jnp.float32, jnp.bfloat16
    dma = pltpu.SemaphoreType.DMA
    hbm = pl.BlockSpec(memory_space=pltpu.HBM)
    smem = pl.BlockSpec(memory_space=pltpu.SMEM)
    field = (tile_rows, nodes, species)
    lists = (directions, capacity, nodes, species)
    product, quad = pl.pallas_call(
        functools.partial(kernel, count, scaling),
        out_shape=(pltpu.VMEM(field, f32), jax.ShapeDtypeStruct((1,), f32)),
        in_specs=[hbm] * 5,
        out_specs=(pl.BlockSpec(memory_space=vmem), smem),
        scratch_shapes=[
            vmem(field, f32),
            vmem(space_tiles.shape, f32),
            vmem(tree_precision.shape, f32),
            pltpu.SMEM((directions, capacity), jnp.int32),
            pltpu.SMEM(column_tiles.shape[::-1], jnp.int32),
            vmem((tile_rows, 2 * nodes, width), bf16),
            vmem((tile_rows + directions * capacity, nodes, 2 * species), bf16),
            vmem((tile_rows + directions * capacity, nodes, species), f32),
            vmem((tile_rows, stored, nodes, species), f32),
            vmem(lists, f32),
            vmem(lists, f32),
            vmem((inner, 8, species), f32),
            vmem((count // inner, 8, species), f32),
            dma,
            dma((3,)),
            dma((CHUNKS,)),
            dma((directions,)),
            dma((directions,)),
            dma((inner,)),
            dma((inner,)),
            dma((count // inner,)),
            dma((count // inner,)),
        ],
        compiler_params=pltpu.CompilerParams(
            collective_id=0, has_side_effects=True, vmem_limit_bytes=40 * 2**20
        ),
        cost_estimate=pl.CostEstimate(
            flops=2 * tile_rows * nodes * species * (width + 2 * species),
            bytes_accessed=4 * (space_tiles.size + 2 * signal.size),
            transcendentals=0,
        ),
        name="kronecker_product",
    )(*(
        pltpu.with_memory_space_constraint(array, pltpu.HBM)
        for array in (signal.reshape(field), space_tiles, tree_precision, send_tiles[0], column_tiles.T)
    ))
    return product.reshape(signal.shape), quad


def solution(mesh):
    placed = (
        P(("groups", "space"), None),
        P("space", None, None),
        P("groups", None),
        P("space", None, None),
        P("space", None),
    )
    return jax.shard_map(
        on_device,
        mesh=mesh,
        in_specs=placed,
        out_specs=(P(("groups", "space"), None), P("groups")),
        check_vma=False,
    )
```

```python
import functools
import math

import jax
import jax.numpy as jnp
from jax import lax
from jax.experimental import pallas as pl
from jax.experimental.pallas import tpu as pltpu
from jax.sharding import PartitionSpec as P

ROWS = 8
CHUNKS = 4
GROUP = 4
MESH = pl.DeviceIdType.MESH


def halves(value):
    high = value.astype(jnp.bfloat16)
    low = (value - high.astype(jnp.float32)).astype(jnp.bfloat16)
    return high, low


def doubled(matrix):
    high, low = halves(matrix)
    zero = jnp.zeros_like(low)
    return jnp.concatenate(
        [jnp.concatenate([high, low], 1), jnp.concatenate([high, zero], 1)], 0
    )


def times(paired, weights):
    both = jnp.dot(paired, weights, preferred_element_type=jnp.float32)
    half = both.shape[1] // 2
    return both[:, :half] + both[:, half:]


def tile_product(stacked, block):
    both = jnp.dot(stacked, block, preferred_element_type=jnp.float32)
    nodes, species = both.shape[0] // 2, both.shape[1] // 2
    small = both[:nodes, species:] + both[nodes:, :species] + both[nodes:, species:]
    return both[:nodes, :species] + small


def rows_product(stacked, columns, xs, z, weights):
    rows, shares = [], []
    for t, row_columns in enumerate(columns):
        block = jnp.concatenate([xs[c] for c in row_columns], 0)
        rows.append(tile_product(stacked[t], block))
        term = z[t] * rows[-1]
        shares.append(jnp.sum(term.reshape(-1, 8, term.shape[-1]), axis=0))
    high, low = halves(jnp.concatenate(rows, 0))
    result = times(jnp.concatenate([high, low], 1), weights)
    return result.reshape(len(rows), -1, result.shape[-1]), shares


def send_and_interior(
    count,
    signal_ref, tiles_ref, tree_ref, send_ref, column_ref,
    product, xs, a, z, shares, weights,
    x, tiles, tree_in, send_in, column_in, outgoing, received,
    x_sem, small_sem, tiles_sem, send_sem, recv_sem,
):
    tile_rows, nodes, species = x.shape
    stored = column_ref.shape[0]
    capacity = send_ref.shape[1]
    load_send = pltpu.make_async_copy(send_ref, send_in, small_sem.at[0])
    load_send.start()
    load_x = pltpu.make_async_copy(signal_ref, x, x_sem)
    load_x.start()
    load_tree = pltpu.make_async_copy(tree_ref, tree_in, small_sem.at[1])
    load_tree.start()
    load_column = pltpu.make_async_copy(column_ref, column_in, small_sem.at[2])
    load_column.start()
    wide = count // ROWS
    me = lax.axis_index("space")
    column, row = lax.rem(me, wide), me // wide
    not_first, not_last = column > 0, column < wide - 1
    above, below = row > 0, row < ROWS - 1
    sends = (not_last, not_first, below, above)
    receives = (not_first, not_last, above, below)
    targets = (me + 1, me - 1, me + wide, me - wide)

    part = tile_rows // CHUNKS
    loads = []
    for c in range(CHUNKS):
        piece = pl.ds(c * part, part)
        loads.append(pltpu.make_async_copy(tiles_ref.at[piece], tiles.at[piece], tiles_sem.at[c]))
        loads[-1].start()

    barrier = pltpu.get_barrier_semaphore()

    def greet(device):
        pl.semaphore_signal(barrier, inc=1, device_id={"space": device}, device_id_type=MESH)

    for d in range(4):
        pl.when(sends[d])(functools.partial(greet, targets[d]))
    greeted = sum(jnp.where(has, 1, 0) for has in receives)

    load_send.wait()
    load_x.wait()

    def copy_for(d):
        return pltpu.make_async_remote_copy(
            src_ref=outgoing.at[d],
            dst_ref=received.at[d],
            send_sem=send_sem.at[d],
            recv_sem=recv_sem.at[d],
            device_id={"space": targets[d]},
            device_id_type=MESH,
        )

    for d in (2, 3, 0, 1):
        for j in range(capacity):
            outgoing[d, j] = x[send_in[d, j]]
        if d == 2:
            pl.semaphore_wait(barrier, greeted)

        @pl.when(sends[d])
        def _():
            copy_for(d).start()

    load_tree.wait()
    tree = tree_in[...]
    right, right_t = doubled(tree), doubled(tree.T)

    weights[...] = right_t
    load_column.wait()

    def prepare(c, carry):
        piece = pl.ds(c * part, part)
        high, low = halves(x[piece])
        paired = jnp.concatenate([high, low], 2)
        xs[piece] = paired
        weighted = times(paired.reshape(part * nodes, 2 * species), right)
        z[piece] = weighted.reshape(part, nodes, species)
        return carry

    lax.fori_loop(0, CHUNKS, prepare, 0)
    for load in loads:
        load.wait()

    def interior(c, carry):
        first = c * part
        piece = pl.ds(first, part)
        high, low = halves(tiles[piece])
        a[piece] = jnp.concatenate([high, low], 1)
        own = [
            [jnp.minimum(column_in[k, first + t], tile_rows - 1) for k in range(stored)]
            for t in range(part)
        ]
        result, sums = rows_product(a.at[piece], own, xs, z.at[piece], right_t)
        product[piece] = result
        for t in range(part):
            shares[first + t] = sums[t]
        return carry

    lax.fori_loop(0, CHUNKS, interior, 0)

    for d in (0, 1, 2, 3):
        @pl.when(receives[d])
        def _():
            copy_for(d).wait_recv()
            for j in range(capacity):
                high, low = halves(received[d, j])
                xs[tile_rows + d * capacity + j] = jnp.concatenate([high, low], 1)
    for d in range(4):
        @pl.when(sends[d])
        def _():
            copy_for(d).wait_send()


def boundary(
    interior, xs, a, z, shares, weights, columns_ref, product_ref, total_ref,
    again, columns, column_sem, out_sem,
):
    tile_rows = interior.shape[0]
    stored = columns.shape[0]
    load = pltpu.make_async_copy(columns_ref, columns, column_sem)
    load.start()
    load.wait()

    def group(g, acc):
        first = g * GROUP
        piece = pl.ds(first, GROUP)
        named = [[columns[k, first + t] for k in range(stored)] for t in range(GROUP)]
        furthest = functools.reduce(jnp.maximum, [c for row in named for c in row])

        def compute():
            result, sums = rows_product(a.at[piece], named, xs, z.at[piece], weights[...])
            again[piece] = result
            pltpu.make_async_copy(again.at[piece], product_ref.at[piece], out_sem).start()
            return functools.reduce(jnp.add, sums)

        def keep():
            pltpu.make_async_copy(interior.at[piece], product_ref.at[piece], out_sem).start()
            return jnp.sum(shares[piece], axis=0)

        return acc + lax.cond(furthest >= tile_rows, compute, keep)

    total_ref[...] = lax.fori_loop(0, tile_rows // GROUP, group, jnp.zeros_like(total_ref))
    pltpu.make_async_copy(again, product_ref, out_sem).wait()


def sum_shares(
    scaling, total_ref, quad_ref,
    inner_shares, outer_shares, inner_send, inner_recv, outer_send, outer_recv,
):
    me = lax.axis_index("space")
    inner, outer = inner_shares.shape[0], outer_shares.shape[0]
    spot, team = lax.rem(me, inner), me // inner
    mates = [team * inner + lax.rem(spot + i, inner) for i in range(1, inner)]
    peers = [spot + inner * lax.rem(team + i, outer) for i in range(1, outer)]

    barrier = pltpu.get_barrier_semaphore()
    for device in mates + peers:
        pl.semaphore_signal(barrier, inc=1, device_id={"space": device}, device_id_type=MESH)

    def share_copies(shares, mine, send, receive, devices):
        return [
            pltpu.make_async_remote_copy(
                src_ref=shares.at[mine],
                dst_ref=shares.at[mine],
                send_sem=send.at[i],
                recv_sem=receive.at[i],
                device_id={"space": device},
                device_id_type=MESH,
            )
            for i, device in enumerate(devices)
        ]

    first = share_copies(inner_shares, spot, inner_send, inner_recv, mates)
    second = share_copies(outer_shares, team, outer_send, outer_recv, peers)
    inner_shares[spot] = total_ref[...]
    pl.semaphore_wait(barrier, len(mates) + len(peers))
    for copy in first:
        copy.start()
    for copy in first:
        copy.wait_recv()
    outer_shares[team] = jnp.sum(inner_shares[...], axis=0)
    for copy in second:
        copy.start()
    for copy in second:
        copy.wait_recv()
    quad_ref[0] = jnp.sum(jnp.sum(outer_shares[...], axis=0)) * scaling
    for copy in first + second:
        copy.wait_send()


def on_device(signal, space_tiles, tree_precision, send_tiles, column_tiles):
    count = lax.axis_size("space")
    tile_rows, nodes, width = space_tiles.shape
    stored = column_tiles.shape[1]
    species = signal.shape[1]
    directions, capacity = send_tiles.shape[1:]
    inner = max(i for i in range(1, math.isqrt(count) + 1) if count % i == 0)
    scaling = 1.0 / math.sqrt(count * tile_rows * nodes * species)
    vmem, f32, bf16 = pltpu.VMEM, jnp.float32, jnp.bfloat16
    dma = pltpu.SemaphoreType.DMA
    hbm = pl.BlockSpec(memory_space=pltpu.HBM)
    near = pl.BlockSpec(memory_space=vmem)
    smem = pl.BlockSpec(memory_space=pltpu.SMEM)
    field = (tile_rows, nodes, species)
    lists = (directions, capacity, nodes, species)
    share = (8, species)
    columns = column_tiles.T
    flops = 2 * tile_rows * nodes * species * (width + 2 * species)
    between = (
        vmem(field, f32),
        vmem((tile_rows + directions * capacity, nodes, 2 * species), bf16),
        vmem((tile_rows, 2 * nodes, width), bf16),
        vmem(field, f32),
        vmem((tile_rows, *share), f32),
        vmem((2 * species, 2 * species), bf16),
    )
    kept = pl.pallas_call(
        functools.partial(send_and_interior, count),
        out_shape=between,
        in_specs=[hbm] * 5,
        out_specs=(near,) * len(between),
        scratch_shapes=[
            vmem(field, f32),
            vmem(space_tiles.shape, f32),
            vmem(tree_precision.shape, f32),
            pltpu.SMEM((directions, capacity), jnp.int32),
            pltpu.SMEM(columns.shape, jnp.int32),
            vmem(lists, f32),
            vmem(lists, f32),
            dma,
            dma((3,)),
            dma((CHUNKS,)),
            dma((directions,)),
            dma((directions,)),
        ],
        compiler_params=pltpu.CompilerParams(
            collective_id=0, has_side_effects=True, vmem_limit_bytes=24 * 2**20
        ),
        cost_estimate=pl.CostEstimate(
            flops=flops, bytes_accessed=4 * (space_tiles.size + signal.size), transcendentals=0
        ),
        name="send_and_interior",
    )(*(
        pltpu.with_memory_space_constraint(array, pltpu.HBM)
        for array in (signal.reshape(field), space_tiles, tree_precision, send_tiles[0], columns)
    ))
    product, total = pl.pallas_call(
        boundary,
        out_shape=(jax.ShapeDtypeStruct(field, f32), vmem(share, f32)),
        in_specs=[near] * len(between) + [hbm],
        out_specs=(hbm, near),
        scratch_shapes=[vmem(field, f32), pltpu.SMEM(columns.shape, jnp.int32), dma, dma],
        compiler_params=pltpu.CompilerParams(vmem_limit_bytes=16 * 2**20),
        cost_estimate=pl.CostEstimate(
            flops=flops, bytes_accessed=4 * signal.size, transcendentals=0
        ),
        name="boundary",
    )(*kept, pltpu.with_memory_space_constraint(columns, pltpu.HBM))
    quad = pl.pallas_call(
        functools.partial(sum_shares, scaling),
        out_shape=jax.ShapeDtypeStruct((1,), f32),
        in_specs=[near],
        out_specs=smem,
        scratch_shapes=[
            vmem((inner, *share), f32),
            vmem((count // inner, *share), f32),
            dma((inner,)),
            dma((inner,)),
            dma((count // inner,)),
            dma((count // inner,)),
        ],
        compiler_params=pltpu.CompilerParams(collective_id=1, has_side_effects=True),
        name="sum_shares",
    )(total)
    return product.reshape(signal.shape), quad


def solution(mesh):
    placed = (
        P(("groups", "space"), None),
        P("space", None, None),
        P("groups", None),
        P("space", None, None),
        P("space", None),
    )
    return jax.shard_map(
        on_device,
        mesh=mesh,
        in_specs=placed,
        out_specs=(P(("groups", "space"), None), P("groups")),
        check_vma=False,
    )
```

```python
import functools
import math

import jax
import jax.numpy as jnp
from jax import lax
from jax.experimental import pallas as pl
from jax.experimental.pallas import tpu as pltpu
from jax.sharding import PartitionSpec as P

ROWS = 8
CHUNKS = 4
GROUP = 4
MESH = pl.DeviceIdType.MESH


def halves(value):
    high = value.astype(jnp.bfloat16)
    low = (value - high.astype(jnp.float32)).astype(jnp.bfloat16)
    return high, low


def doubled(matrix):
    high, low = halves(matrix)
    zero = jnp.zeros_like(low)
    return jnp.concatenate(
        [jnp.concatenate([high, low], 1), jnp.concatenate([high, zero], 1)], 0
    )


def times(paired, weights):
    both = jnp.dot(paired, weights, preferred_element_type=jnp.float32)
    half = both.shape[1] // 2
    return both[:, :half] + both[:, half:]


def tile_product(stacked, block):
    both = jnp.dot(stacked, block, preferred_element_type=jnp.float32)
    nodes, species = both.shape[0] // 2, both.shape[1] // 2
    small = both[:nodes, species:] + both[nodes:, :species] + both[nodes:, species:]
    return both[:nodes, :species] + small


def rows_product(stacked, columns, xs, weights):
    rows = []
    for t, row_columns in enumerate(columns):
        block = jnp.concatenate([xs[c] for c in row_columns], 0)
        rows.append(tile_product(stacked[t], block))
    high, low = halves(jnp.concatenate(rows, 0))
    result = times(jnp.concatenate([high, low], 1), weights)
    return result.reshape(len(rows), -1, result.shape[-1])


def send_and_interior(
    count, scaling,
    signal_ref, tiles_ref, tree_ref, send_ref, column_ref,
    product, xs, a, weights, quad_ref,
    x, tiles, tree_in, send_in, column_in, extended, pull, outgoing, received, shares,
    x_sem, small_sem, tiles_sem, send_sem, recv_sem, share_send, share_recv,
):
    tile_rows, nodes, species = x.shape
    stored = column_ref.shape[0]
    capacity = send_ref.shape[1]
    load_send = pltpu.make_async_copy(send_ref, send_in, small_sem.at[0])
    load_send.start()
    load_x = pltpu.make_async_copy(signal_ref, x, x_sem)
    load_x.start()
    load_tree = pltpu.make_async_copy(tree_ref, tree_in, small_sem.at[1])
    load_tree.start()
    load_column = pltpu.make_async_copy(column_ref, column_in, small_sem.at[2])
    load_column.start()
    wide = count // ROWS
    me = lax.axis_index("space")
    column, row = lax.rem(me, wide), me // wide
    not_first, not_last = column > 0, column < wide - 1
    above, below = row > 0, row < ROWS - 1
    sends = (not_last, not_first, below, above)
    receives = (not_first, not_last, above, below)
    targets = (me + 1, me - 1, me + wide, me - wide)

    part = tile_rows // CHUNKS
    loads = []
    for c in range(CHUNKS):
        piece = pl.ds(c * part, part)
        loads.append(pltpu.make_async_copy(tiles_ref.at[piece], tiles.at[piece], tiles_sem.at[c]))
        loads[-1].start()

    barrier = pltpu.get_barrier_semaphore()

    others = [lax.rem(me + i, count) for i in range(1, count)]
    for device in others:
        pl.semaphore_signal(barrier, inc=1, device_id={"space": device}, device_id_type=MESH)

    load_send.wait()
    load_x.wait()

    def copy_for(d):
        return pltpu.make_async_remote_copy(
            src_ref=outgoing.at[d],
            dst_ref=received.at[d],
            send_sem=send_sem.at[d],
            recv_sem=recv_sem.at[d],
            device_id={"space": targets[d]},
            device_id_type=MESH,
        )

    for d in (2, 3, 0, 1):
        for j in range(capacity):
            outgoing[d, j] = x[send_in[d, j]]
        if d == 2:
            pl.semaphore_wait(barrier, count - 1)

        @pl.when(sends[d])
        def _():
            copy_for(d).start()

    load_tree.wait()
    tree = tree_in[...]
    right, right_t = doubled(tree), doubled(tree.T)

    weights[...] = right_t
    load_column.wait()

    for load in loads:
        load.wait()

    def prepare(c, carry):
        piece = pl.ds(c * part, part)
        own = x[piece]
        extended[piece] = own
        high, low = halves(own)
        paired = jnp.concatenate([high, low], 2)
        xs[piece] = paired
        weighted = times(paired.reshape(part * nodes, 2 * species), right)
        weighted = weighted.reshape(part, nodes, species)
        for i in range(part):
            t = c * part + i
            high, low = halves(tiles[t])
            stacked = jnp.concatenate([high, low], 0)
            a[t] = stacked
            high, low = halves(weighted[i])
            high_low = jnp.concatenate([high, low], 1)
            both = lax.dot_general(
                stacked,
                jnp.concatenate([high_low, high_low], 0),
                (((0,), (0,)), ((), ())),
                preferred_element_type=jnp.float32,
            )
            pull[t] = (both[:, :species] + both[:, species:]).reshape(stored, nodes, species)
        return carry

    lax.fori_loop(0, CHUNKS, prepare, 0)

    def multiply(c, last):
        first = c * part
        piece = pl.ds(first, part)
        named = [
            [jnp.minimum(column_in[k, first + t], last) for k in range(stored)]
            for t in range(part)
        ]
        product[piece] = rows_product(a.at[piece], named, xs, right_t)

    def interior(c, carry):
        multiply(c, tile_rows - 1)
        return carry

    lax.fori_loop(CHUNKS // 2, CHUNKS, interior, 0)

    for d in (0, 1, 2, 3):
        @pl.when(receives[d])
        def _():
            copy_for(d).wait_recv()
            for j in range(capacity):
                tile = received[d, j]
                extended[tile_rows + d * capacity + j] = tile
                high, low = halves(tile)
                xs[tile_rows + d * capacity + j] = jnp.concatenate([high, low], 1)

    def weigh(t, acc):
        for k in range(stored):
            term = pull[t, k] * extended[column_in[k, t]]
            acc = acc + jnp.sum(term.reshape(nodes // 8, 8, species), axis=0)
        return acc

    shares[me] = lax.fori_loop(
        0, tile_rows, weigh, jnp.zeros((8, species), jnp.float32), unroll=4
    )
    copies = [
        pltpu.make_async_remote_copy(
            src_ref=shares.at[me],
            dst_ref=shares.at[me],
            send_sem=share_send.at[i],
            recv_sem=share_recv.at[i],
            device_id={"space": device},
            device_id_type=MESH,
        )
        for i, device in enumerate(others)
    ]
    for copy in copies:
        copy.start()

    def full(c, carry):
        multiply(c, xs.shape[0] - 1)
        return carry

    lax.fori_loop(0, CHUNKS // 2, full, 0)

    for d in range(4):
        @pl.when(sends[d])
        def _():
            copy_for(d).wait_send()
    for copy in copies:
        copy.wait_recv()
    quad_ref[0] = jnp.sum(jnp.sum(shares[...], axis=0)) * scaling
    for copy in copies:
        copy.wait_send()


def boundary(
    done, interior, xs, a, weights, columns_ref, product_ref, again, columns, column_sem, out_sem,
):
    tile_rows = interior.shape[0]
    stored = columns.shape[0]
    load = pltpu.make_async_copy(columns_ref, columns, column_sem)
    load.start()
    final = pl.ds(0, done)
    pltpu.make_async_copy(interior.at[final], product_ref.at[final], out_sem).start()
    load.wait()

    def group(g, carry):
        first = g * GROUP
        piece = pl.ds(first, GROUP)
        named = [[columns[k, first + t] for k in range(stored)] for t in range(GROUP)]
        furthest = functools.reduce(jnp.maximum, [c for row in named for c in row])

        @pl.when(furthest >= tile_rows)
        def _():
            again[piece] = rows_product(a.at[piece], named, xs, weights[...])
            pltpu.make_async_copy(again.at[piece], product_ref.at[piece], out_sem).start()

        @pl.when(furthest < tile_rows)
        def _():
            pltpu.make_async_copy(interior.at[piece], product_ref.at[piece], out_sem).start()

        return carry

    lax.fori_loop(done // GROUP, tile_rows // GROUP, group, 0)
    pltpu.make_async_copy(again, product_ref, out_sem).wait()


def on_device(signal, space_tiles, tree_precision, send_tiles, column_tiles):
    count = lax.axis_size("space")
    tile_rows, nodes, width = space_tiles.shape
    stored = column_tiles.shape[1]
    species = signal.shape[1]
    directions, capacity = send_tiles.shape[1:]
    scaling = 1.0 / math.sqrt(count * tile_rows * nodes * species)
    vmem, f32, bf16 = pltpu.VMEM, jnp.float32, jnp.bfloat16
    dma = pltpu.SemaphoreType.DMA
    hbm = pl.BlockSpec(memory_space=pltpu.HBM)
    near = pl.BlockSpec(memory_space=vmem)
    smem = pl.BlockSpec(memory_space=pltpu.SMEM)
    field = (tile_rows, nodes, species)
    lists = (directions, capacity, nodes, species)
    columns = column_tiles.T
    flops = 2 * tile_rows * nodes * species * (width + 2 * species)
    between = (
        vmem(field, f32),
        vmem((tile_rows + directions * capacity, nodes, 2 * species), bf16),
        vmem((tile_rows, 2 * nodes, width), bf16),
        vmem((2 * species, 2 * species), bf16),
    )
    *kept, quad = pl.pallas_call(
        functools.partial(send_and_interior, count, scaling),
        out_shape=(*between, jax.ShapeDtypeStruct((1,), f32)),
        in_specs=[hbm] * 5,
        out_specs=(near,) * len(between) + (smem,),
        scratch_shapes=[
            vmem(field, f32),
            vmem(space_tiles.shape, f32),
            vmem(tree_precision.shape, f32),
            pltpu.SMEM((directions, capacity), jnp.int32),
            pltpu.SMEM(columns.shape, jnp.int32),
            vmem((tile_rows + directions * capacity, nodes, species), f32),
            vmem((tile_rows, stored, nodes, species), f32),
            vmem(lists, f32),
            vmem(lists, f32),
            vmem((count, 8, species), f32),
            dma,
            dma((3,)),
            dma((CHUNKS,)),
            dma((directions,)),
            dma((directions,)),
            dma((count,)),
            dma((count,)),
        ],
        compiler_params=pltpu.CompilerParams(
            collective_id=0, has_side_effects=True, vmem_limit_bytes=32 * 2**20
        ),
        cost_estimate=pl.CostEstimate(
            flops=flops, bytes_accessed=4 * (space_tiles.size + signal.size), transcendentals=0
        ),
        name="send_and_interior",
    )(*(
        pltpu.with_memory_space_constraint(array, pltpu.HBM)
        for array in (signal.reshape(field), space_tiles, tree_precision, send_tiles[0], columns)
    ))
    product = pl.pallas_call(
        functools.partial(boundary, tile_rows // CHUNKS * (CHUNKS // 2)),
        out_shape=jax.ShapeDtypeStruct(field, f32),
        in_specs=[near] * len(between) + [hbm],
        out_specs=hbm,
        scratch_shapes=[vmem(field, f32), pltpu.SMEM(columns.shape, jnp.int32), dma, dma],
        compiler_params=pltpu.CompilerParams(vmem_limit_bytes=16 * 2**20),
        cost_estimate=pl.CostEstimate(
            flops=flops, bytes_accessed=4 * signal.size, transcendentals=0
        ),
        name="boundary",
    )(*kept, pltpu.with_memory_space_constraint(columns, pltpu.HBM))
    return product.reshape(signal.shape), quad


def solution(mesh):
    placed = (
        P(("groups", "space"), None),
        P("space", None, None),
        P("groups", None),
        P("space", None, None),
        P("space", None),
    )
    return jax.shard_map(
        on_device,
        mesh=mesh,
        in_specs=placed,
        out_specs=(P(("groups", "space"), None), P("groups")),
        check_vma=False,
    )
```

```python
import functools
import math

import jax
import jax.numpy as jnp
from jax import lax
from jax.experimental import pallas as pl
from jax.experimental.pallas import tpu as pltpu
from jax.sharding import PartitionSpec as P

ROWS = 8
CHUNKS = 4
FULL = 3
GROUP = 4
MESH = pl.DeviceIdType.MESH


def halves(value):
    high = value.astype(jnp.bfloat16)
    low = (value - high.astype(jnp.float32)).astype(jnp.bfloat16)
    return high, low


def doubled(matrix):
    high, low = halves(matrix)
    zero = jnp.zeros_like(low)
    return jnp.concatenate(
        [jnp.concatenate([high, low], 1), jnp.concatenate([high, zero], 1)], 0
    )


def apart(one, two):
    zero = jnp.zeros_like(one)
    return jnp.concatenate(
        [jnp.concatenate([one, zero], 1), jnp.concatenate([zero, two], 1)], 0
    )


def times(paired, weights):
    both = jnp.dot(paired, weights, preferred_element_type=jnp.float32)
    half = both.shape[1] // 2
    return both[:, :half] + both[:, half:]


def tile_product(stacked, block):
    both = jnp.dot(stacked, block, preferred_element_type=jnp.float32)
    nodes, species = both.shape[0] // 2, both.shape[1] // 2
    small = both[:nodes, species:] + both[nodes:, :species] + both[nodes:, species:]
    return both[:nodes, :species] + small


def rows_product(stacked, columns, xs, weights):
    rows = []
    for t, row_columns in enumerate(columns):
        block = jnp.concatenate([xs[c] for c in row_columns], 0)
        rows.append(tile_product(stacked[t], block))
    high, low = halves(jnp.concatenate(rows, 0))
    result = times(jnp.concatenate([high, low], 1), weights)
    return result.reshape(len(rows), -1, result.shape[-1])


def send_and_interior(
    count, scaling,
    signal_ref, tiles_ref, tree_ref, send_ref, column_ref,
    product, xs, a, weights, quad_ref,
    x, tiles, tree_in, send_in, column_in, extended, pull, outgoing, received, shares,
    x_sem, small_sem, tiles_sem, send_sem, recv_sem, share_send, share_recv,
):
    tile_rows, nodes, species = x.shape
    stored = column_ref.shape[0]
    capacity = send_ref.shape[1]
    load_send = pltpu.make_async_copy(send_ref, send_in, small_sem.at[0])
    load_send.start()
    load_x = pltpu.make_async_copy(signal_ref, x, x_sem)
    load_x.start()
    load_tree = pltpu.make_async_copy(tree_ref, tree_in, small_sem.at[1])
    load_tree.start()
    load_column = pltpu.make_async_copy(column_ref, column_in, small_sem.at[2])
    load_column.start()
    wide = count // ROWS
    me = lax.axis_index("space")
    column, row = lax.rem(me, wide), me // wide
    not_first, not_last = column > 0, column < wide - 1
    above, below = row > 0, row < ROWS - 1
    sends = (not_last, not_first, below, above)
    receives = (not_first, not_last, above, below)
    targets = (me + 1, me - 1, me + wide, me - wide)

    part = tile_rows // CHUNKS
    loads = []
    for c in range(CHUNKS):
        piece = pl.ds(c * part, part)
        loads.append(pltpu.make_async_copy(tiles_ref.at[piece], tiles.at[piece], tiles_sem.at[c]))
        loads[-1].start()

    barrier = pltpu.get_barrier_semaphore()

    others = [lax.rem(me + i, count) for i in range(1, count)]
    for device in others:
        pl.semaphore_signal(barrier, inc=1, device_id={"space": device}, device_id_type=MESH)

    load_send.wait()
    load_x.wait()

    def copy_for(d):
        return pltpu.make_async_remote_copy(
            src_ref=outgoing.at[d],
            dst_ref=received.at[d],
            send_sem=send_sem.at[d],
            recv_sem=recv_sem.at[d],
            device_id={"space": targets[d]},
            device_id_type=MESH,
        )

    for d in (2, 3, 0, 1):
        for j in range(capacity):
            outgoing[d, j] = x[send_in[d, j]]
        if d == 2:
            pl.semaphore_wait(barrier, count - 1)

        @pl.when(sends[d])
        def _():
            copy_for(d).start()

    load_tree.wait()
    tree = tree_in[...]
    right, right_t = doubled(tree), doubled(tree.T)

    weights[...] = right_t
    load_column.wait()

    for load in loads:
        load.wait()

    def prepare(c, carry):
        piece = pl.ds(c * part, part)
        own = x[piece]
        extended[piece] = own
        high, low = halves(own)
        paired = jnp.concatenate([high, low], 2)
        xs[piece] = paired
        weighted = times(paired.reshape(part * nodes, 2 * species), right)
        weighted = weighted.reshape(part, nodes, species)
        z_high, z_low = halves(weighted)
        for i in range(part):
            t = c * part + i
            high, low = halves(tiles[t])
            a[t] = jnp.concatenate([high, low], 0)
        for i in range(0, part, 2):
            t = c * part + i
            turned = tiles[pl.ds(t, 2)].reshape(2 * nodes, stored * nodes).T
            high, low = halves(turned)
            both = jnp.dot(
                jnp.concatenate([high, low, high], 1),
                jnp.concatenate(
                    [apart(z_high[i], z_high[i + 1])] * 2 + [apart(z_low[i], z_low[i + 1])], 0
                ),
                preferred_element_type=jnp.float32,
            )
            for j in range(2):
                mine = both[:, j * species : (j + 1) * species]
                pull[t + j] = mine.reshape(stored, nodes, species)
        return carry

    lax.fori_loop(0, CHUNKS, prepare, 0)

    def multiply(c, last):
        first = c * part
        piece = pl.ds(first, part)
        named = [
            [jnp.minimum(column_in[k, first + t], last) for k in range(stored)]
            for t in range(part)
        ]
        product[piece] = rows_product(a.at[piece], named, xs, right_t)

    def interior(c, carry):
        multiply(c, tile_rows - 1)
        return carry

    lax.fori_loop(FULL, CHUNKS, interior, 0)

    for d in (0, 1, 2, 3):
        @pl.when(receives[d])
        def _():
            copy_for(d).wait_recv()
            for j in range(capacity):
                tile = received[d, j]
                extended[tile_rows + d * capacity + j] = tile
                high, low = halves(tile)
                xs[tile_rows + d * capacity + j] = jnp.concatenate([high, low], 1)

    def weigh(t, acc):
        for k in range(stored):
            term = pull[t, k] * extended[column_in[k, t]]
            acc = acc + jnp.sum(term.reshape(nodes // 8, 8, species), axis=0)
        return acc

    shares[me] = lax.fori_loop(
        0, tile_rows, weigh, jnp.zeros((8, species), jnp.float32), unroll=4
    )
    copies = [
        pltpu.make_async_remote_copy(
            src_ref=shares.at[me],
            dst_ref=shares.at[me],
            send_sem=share_send.at[i],
            recv_sem=share_recv.at[i],
            device_id={"space": device},
            device_id_type=MESH,
        )
        for i, device in enumerate(others)
    ]
    for copy in copies:
        copy.start()

    def full(c, carry):
        multiply(c, xs.shape[0] - 1)
        return carry

    lax.fori_loop(0, FULL, full, 0)

    for d in range(4):
        @pl.when(sends[d])
        def _():
            copy_for(d).wait_send()
    for copy in copies:
        copy.wait_recv()
    quad_ref[0] = jnp.sum(jnp.sum(shares[...], axis=0)) * scaling
    for copy in copies:
        copy.wait_send()


def boundary(
    done, interior, xs, a, weights, columns_ref, product_ref, again, columns, column_sem, out_sem,
):
    tile_rows = interior.shape[0]
    stored = columns.shape[0]
    load = pltpu.make_async_copy(columns_ref, columns, column_sem)
    load.start()
    final = pl.ds(0, done)
    pltpu.make_async_copy(interior.at[final], product_ref.at[final], out_sem).start()
    load.wait()

    def group(g, carry):
        first = g * GROUP
        piece = pl.ds(first, GROUP)
        named = [[columns[k, first + t] for k in range(stored)] for t in range(GROUP)]
        furthest = functools.reduce(jnp.maximum, [c for row in named for c in row])

        @pl.when(furthest >= tile_rows)
        def _():
            again[piece] = rows_product(a.at[piece], named, xs, weights[...])
            pltpu.make_async_copy(again.at[piece], product_ref.at[piece], out_sem).start()

        @pl.when(furthest < tile_rows)
        def _():
            pltpu.make_async_copy(interior.at[piece], product_ref.at[piece], out_sem).start()

        return carry

    lax.fori_loop(done // GROUP, tile_rows // GROUP, group, 0)
    pltpu.make_async_copy(again, product_ref, out_sem).wait()


def on_device(signal, space_tiles, tree_precision, send_tiles, column_tiles):
    count = lax.axis_size("space")
    tile_rows, nodes, width = space_tiles.shape
    stored = column_tiles.shape[1]
    species = signal.shape[1]
    directions, capacity = send_tiles.shape[1:]
    scaling = 1.0 / math.sqrt(count * tile_rows * nodes * species)
    vmem, f32, bf16 = pltpu.VMEM, jnp.float32, jnp.bfloat16
    dma = pltpu.SemaphoreType.DMA
    hbm = pl.BlockSpec(memory_space=pltpu.HBM)
    near = pl.BlockSpec(memory_space=vmem)
    smem = pl.BlockSpec(memory_space=pltpu.SMEM)
    field = (tile_rows, nodes, species)
    lists = (directions, capacity, nodes, species)
    columns = column_tiles.T
    flops = 2 * tile_rows * nodes * species * (width + 2 * species)
    between = (
        vmem(field, f32),
        vmem((tile_rows + directions * capacity, nodes, 2 * species), bf16),
        vmem((tile_rows, 2 * nodes, width), bf16),
        vmem((2 * species, 2 * species), bf16),
    )
    *kept, quad = pl.pallas_call(
        functools.partial(send_and_interior, count, scaling),
        out_shape=(*between, jax.ShapeDtypeStruct((1,), f32)),
        in_specs=[hbm] * 5,
        out_specs=(near,) * len(between) + (smem,),
        scratch_shapes=[
            vmem(field, f32),
            vmem(space_tiles.shape, f32),
            vmem(tree_precision.shape, f32),
            pltpu.SMEM((directions, capacity), jnp.int32),
            pltpu.SMEM(columns.shape, jnp.int32),
            vmem((tile_rows + directions * capacity, nodes, species), f32),
            vmem((tile_rows, stored, nodes, species), f32),
            vmem(lists, f32),
            vmem(lists, f32),
            vmem((count, 8, species), f32),
            dma,
            dma((3,)),
            dma((CHUNKS,)),
            dma((directions,)),
            dma((directions,)),
            dma((count,)),
            dma((count,)),
        ],
        compiler_params=pltpu.CompilerParams(
            collective_id=0, has_side_effects=True, vmem_limit_bytes=32 * 2**20
        ),
        cost_estimate=pl.CostEstimate(
            flops=flops, bytes_accessed=4 * (space_tiles.size + signal.size), transcendentals=0
        ),
        name="send_and_interior",
    )(*(
        pltpu.with_memory_space_constraint(array, pltpu.HBM)
        for array in (signal.reshape(field), space_tiles, tree_precision, send_tiles[0], columns)
    ))
    product = pl.pallas_call(
        functools.partial(boundary, tile_rows // CHUNKS * FULL),
        out_shape=jax.ShapeDtypeStruct(field, f32),
        in_specs=[near] * len(between) + [hbm],
        out_specs=hbm,
        scratch_shapes=[vmem(field, f32), pltpu.SMEM(columns.shape, jnp.int32), dma, dma],
        compiler_params=pltpu.CompilerParams(vmem_limit_bytes=16 * 2**20),
        cost_estimate=pl.CostEstimate(
            flops=flops, bytes_accessed=4 * signal.size, transcendentals=0
        ),
        name="boundary",
    )(*kept, pltpu.with_memory_space_constraint(columns, pltpu.HBM))
    return product.reshape(signal.shape), quad


def solution(mesh):
    placed = (
        P(("groups", "space"), None),
        P("space", None, None),
        P("groups", None),
        P("space", None, None),
        P("space", None),
    )
    return jax.shard_map(
        on_device,
        mesh=mesh,
        in_specs=placed,
        out_specs=(P(("groups", "space"), None), P("groups")),
        check_vma=False,
    )
```

```python
import functools
import math

import jax
import jax.numpy as jnp
from jax import lax
from jax.experimental import pallas as pl
from jax.experimental.pallas import tpu as pltpu
from jax.sharding import PartitionSpec as P

ROWS = 8
CHUNKS = 4
MESH = pl.DeviceIdType.MESH


def halves(value):
    high = value.astype(jnp.bfloat16)
    low = (value - high.astype(jnp.float32)).astype(jnp.bfloat16)
    return high, low


def doubled(matrix):
    high, low = halves(matrix)
    zero = jnp.zeros_like(low)
    return jnp.concatenate(
        [jnp.concatenate([high, low], 1), jnp.concatenate([high, zero], 1)], 0
    )


def apart(one, two):
    zero = jnp.zeros_like(one)
    return jnp.concatenate(
        [jnp.concatenate([one, zero], 1), jnp.concatenate([zero, two], 1)], 0
    )


def times(paired, weights):
    both = jnp.dot(paired, weights, preferred_element_type=jnp.float32)
    half = both.shape[1] // 2
    return both[:, :half] + both[:, half:]


def tile_product(stacked, block):
    both = jnp.dot(stacked, block, preferred_element_type=jnp.float32)
    nodes, species = both.shape[0] // 2, both.shape[1] // 2
    small = both[:nodes, species:] + both[nodes:, :species] + both[nodes:, species:]
    return both[:nodes, :species] + small


def rows_product(stacked, columns, xs, weights):
    rows = []
    for t, row_columns in enumerate(columns):
        block = jnp.concatenate([xs[c] for c in row_columns], 0)
        rows.append(tile_product(stacked[t], block))
    high, low = halves(jnp.concatenate(rows, 0))
    result = times(jnp.concatenate([high, low], 1), weights)
    return result.reshape(len(rows), -1, result.shape[-1])


def kronecker_product(
    count, scaling,
    signal_ref, tiles_ref, tree_ref, send_ref, column_ref,
    product, quad_ref,
    x, tiles, tree_in, send_in, column_in, xs, a, extended, pull, outgoing, received, shares,
    x_sem, small_sem, tiles_sem, send_sem, recv_sem, share_send, share_recv,
):
    tile_rows, nodes, species = x.shape
    stored = column_ref.shape[0]
    capacity = send_ref.shape[1]
    load_send = pltpu.make_async_copy(send_ref, send_in, small_sem.at[0])
    load_send.start()
    load_x = pltpu.make_async_copy(signal_ref, x, x_sem)
    load_x.start()
    load_tree = pltpu.make_async_copy(tree_ref, tree_in, small_sem.at[1])
    load_column = pltpu.make_async_copy(column_ref, column_in, small_sem.at[2])
    wide = count // ROWS
    me = lax.axis_index("space")
    column, row = lax.rem(me, wide), me // wide
    not_first, not_last = column > 0, column < wide - 1
    above, below = row > 0, row < ROWS - 1
    sends = (not_last, not_first, below, above)
    receives = (not_first, not_last, above, below)
    targets = (me + 1, me - 1, me + wide, me - wide)

    part = tile_rows // CHUNKS
    loads = []
    for c in range(CHUNKS):
        piece = pl.ds(c * part, part)
        loads.append(pltpu.make_async_copy(tiles_ref.at[piece], tiles.at[piece], tiles_sem.at[c]))

    barrier = pltpu.get_barrier_semaphore()

    others = [lax.rem(me + i, count) for i in range(1, count)]
    for device in others:
        pl.semaphore_signal(barrier, inc=1, device_id={"space": device}, device_id_type=MESH)

    load_send.wait()
    load_x.wait()
    load_tree.start()
    load_column.start()
    for load in loads:
        load.start()

    def copy_for(d):
        return pltpu.make_async_remote_copy(
            src_ref=outgoing.at[d],
            dst_ref=received.at[d],
            send_sem=send_sem.at[d],
            recv_sem=recv_sem.at[d],
            device_id={"space": targets[d]},
            device_id_type=MESH,
        )

    for d in (2, 3, 0, 1):
        for j in range(capacity):
            outgoing[d, j] = x[send_in[d, j]]
        if d == 2:
            pl.semaphore_wait(barrier, count - 1)

        @pl.when(sends[d])
        def _():
            copy_for(d).start()

    load_tree.wait()
    tree = tree_in[...]
    right, right_t = doubled(tree), doubled(tree.T)

    load_column.wait()

    for load in loads:
        load.wait()

    def prepare(c, carry):
        piece = pl.ds(c * part, part)
        own = x[piece]
        extended[piece] = own
        high, low = halves(own)
        paired = jnp.concatenate([high, low], 2)
        xs[piece] = paired
        weighted = times(paired.reshape(part * nodes, 2 * species), right)
        weighted = weighted.reshape(part, nodes, species)
        z_high, z_low = halves(weighted)
        for i in range(part):
            t = c * part + i
            high, low = halves(tiles[t])
            a[t] = jnp.concatenate([high, low], 0)
        for i in range(0, part, 2):
            t = c * part + i
            turned = tiles[pl.ds(t, 2)].reshape(2 * nodes, stored * nodes).T
            high, low = halves(turned)
            both = jnp.dot(
                jnp.concatenate([high, low, high], 1),
                jnp.concatenate(
                    [apart(z_high[i], z_high[i + 1])] * 2 + [apart(z_low[i], z_low[i + 1])], 0
                ),
                preferred_element_type=jnp.float32,
            )
            for j in range(2):
                mine = both[:, j * species : (j + 1) * species]
                pull[t + j] = mine.reshape(stored, nodes, species)
        return carry

    lax.fori_loop(0, CHUNKS, prepare, 0)

    for d in (0, 1, 2, 3):
        @pl.when(receives[d])
        def _():
            copy_for(d).wait_recv()
            for j in range(capacity):
                tile = received[d, j]
                extended[tile_rows + d * capacity + j] = tile
                high, low = halves(tile)
                xs[tile_rows + d * capacity + j] = jnp.concatenate([high, low], 1)

    def weigh(t, acc):
        for k in range(stored):
            term = pull[t, k] * extended[column_in[k, t]]
            acc = acc + jnp.sum(term.reshape(nodes // 8, 8, species), axis=0)
        return acc

    shares[me] = lax.fori_loop(
        0, tile_rows, weigh, jnp.zeros((8, species), jnp.float32), unroll=4
    )
    copies = [
        pltpu.make_async_remote_copy(
            src_ref=shares.at[me],
            dst_ref=shares.at[me],
            send_sem=share_send.at[i],
            recv_sem=share_recv.at[i],
            device_id={"space": device},
            device_id_type=MESH,
        )
        for i, device in enumerate(others)
    ]
    for copy in copies:
        copy.start()

    def multiply(c, carry):
        first = c * part
        piece = pl.ds(first, part)
        named = [[column_in[k, first + t] for k in range(stored)] for t in range(part)]
        product[piece] = rows_product(a.at[piece], named, xs, right_t)
        return carry

    lax.fori_loop(0, CHUNKS, multiply, 0)

    for d in range(4):
        @pl.when(sends[d])
        def _():
            copy_for(d).wait_send()
    for copy in copies:
        copy.wait_recv()
    quad_ref[0] = jnp.sum(jnp.sum(shares[...], axis=0)) * scaling
    for copy in copies:
        copy.wait_send()


def on_device(signal, space_tiles, tree_precision, send_tiles, column_tiles):
    count = lax.axis_size("space")
    tile_rows, nodes, width = space_tiles.shape
    stored = column_tiles.shape[1]
    species = signal.shape[1]
    directions, capacity = send_tiles.shape[1:]
    scaling = 1.0 / math.sqrt(count * tile_rows * nodes * species)
    vmem, f32, bf16 = pltpu.VMEM, jnp.float32, jnp.bfloat16
    dma = pltpu.SemaphoreType.DMA
    hbm = pl.BlockSpec(memory_space=pltpu.HBM)
    near = pl.BlockSpec(memory_space=vmem)
    smem = pl.BlockSpec(memory_space=pltpu.SMEM)
    field = (tile_rows, nodes, species)
    lists = (directions, capacity, nodes, species)
    columns = column_tiles.T
    flops = 2 * tile_rows * nodes * species * (width + 2 * species)
    product, quad = pl.pallas_call(
        functools.partial(kronecker_product, count, scaling),
        out_shape=(vmem(field, f32), jax.ShapeDtypeStruct((1,), f32)),
        in_specs=[hbm] * 5,
        out_specs=(near, smem),
        scratch_shapes=[
            vmem(field, f32),
            vmem(space_tiles.shape, f32),
            vmem(tree_precision.shape, f32),
            pltpu.SMEM((directions, capacity), jnp.int32),
            pltpu.SMEM(columns.shape, jnp.int32),
            vmem((tile_rows + directions * capacity, nodes, 2 * species), bf16),
            vmem((tile_rows, 2 * nodes, width), bf16),
            vmem((tile_rows + directions * capacity, nodes, species), f32),
            vmem((tile_rows, stored, nodes, species), f32),
            vmem(lists, f32),
            vmem(lists, f32),
            vmem((count, 8, species), f32),
            dma,
            dma((3,)),
            dma((CHUNKS,)),
            dma((directions,)),
            dma((directions,)),
            dma((count,)),
            dma((count,)),
        ],
        compiler_params=pltpu.CompilerParams(
            collective_id=0, has_side_effects=True, vmem_limit_bytes=40 * 2**20
        ),
        cost_estimate=pl.CostEstimate(
            flops=flops, bytes_accessed=4 * (space_tiles.size + signal.size), transcendentals=0
        ),
        name="kronecker_product",
    )(*(
        pltpu.with_memory_space_constraint(array, pltpu.HBM)
        for array in (signal.reshape(field), space_tiles, tree_precision, send_tiles[0], columns)
    ))
    return product.reshape(signal.shape), quad


def solution(mesh):
    placed = (
        P(("groups", "space"), None),
        P("space", None, None),
        P("groups", None),
        P("space", None, None),
        P("space", None),
    )
    return jax.shard_map(
        on_device,
        mesh=mesh,
        in_specs=placed,
        out_specs=(P(("groups", "space"), None), P("groups")),
        check_vma=False,
    )
```

```python
import functools
import math

import jax
import jax.numpy as jnp
from jax import lax
from jax.experimental import pallas as pl
from jax.experimental.pallas import tpu as pltpu
from jax.sharding import PartitionSpec as P

ROWS = 8
CHUNKS = 4
PIECES = 4
MESH = pl.DeviceIdType.MESH


def halves(value):
    high = value.astype(jnp.bfloat16)
    low = (value - high.astype(jnp.float32)).astype(jnp.bfloat16)
    return high, low


def doubled(matrix):
    high, low = halves(matrix)
    zero = jnp.zeros_like(low)
    return jnp.concatenate(
        [jnp.concatenate([high, low], 1), jnp.concatenate([high, zero], 1)], 0
    )


def apart(one, two):
    zero = jnp.zeros_like(one)
    return jnp.concatenate(
        [jnp.concatenate([one, zero], 1), jnp.concatenate([zero, two], 1)], 0
    )


def times(paired, weights):
    both = jnp.dot(paired, weights, preferred_element_type=jnp.float32)
    half = both.shape[1] // 2
    return both[:, :half] + both[:, half:]


def tile_product(stacked, block):
    both = jnp.dot(stacked, block, preferred_element_type=jnp.float32)
    nodes, species = both.shape[0] // 2, both.shape[1] // 2
    small = both[:nodes, species:] + both[nodes:, :species] + both[nodes:, species:]
    return both[:nodes, :species] + small


def rows_product(stacked, columns, xs, weights):
    rows = []
    for t, row_columns in enumerate(columns):
        block = jnp.concatenate([xs[c] for c in row_columns], 0)
        rows.append(tile_product(stacked[t], block))
    high, low = halves(jnp.concatenate(rows, 0))
    result = times(jnp.concatenate([high, low], 1), weights)
    return result.reshape(len(rows), -1, result.shape[-1])


def kronecker_product(
    count, scaling,
    signal_ref, tiles_ref, tree_ref, send_ref, column_ref,
    product, quad_ref,
    x, tiles, tree_in, send_in, column_in, xs, a, extended, pull, outgoing, received, shares,
    x_sem, small_sem, tiles_sem, send_sem, recv_sem, share_send, share_recv,
):
    tile_rows, nodes, species = x.shape
    stored = column_ref.shape[0]
    capacity = send_ref.shape[1]
    load_send = pltpu.make_async_copy(send_ref, send_in, small_sem.at[0])
    load_send.start()
    load_x = pltpu.make_async_copy(signal_ref, x, x_sem)
    load_x.start()
    load_tree = pltpu.make_async_copy(tree_ref, tree_in, small_sem.at[1])
    load_column = pltpu.make_async_copy(column_ref, column_in, small_sem.at[2])
    wide = count // ROWS
    me = lax.axis_index("space")
    column, row = lax.rem(me, wide), me // wide
    not_first, not_last = column > 0, column < wide - 1
    above, below = row > 0, row < ROWS - 1
    sends = (not_last, not_first, below, above)
    receives = (not_first, not_last, above, below)
    targets = (me + 1, me - 1, me + wide, me - wide)

    part = tile_rows // CHUNKS
    loads = []
    for c in range(CHUNKS):
        piece = pl.ds(c * part, part)
        loads.append(pltpu.make_async_copy(tiles_ref.at[piece], tiles.at[piece], tiles_sem.at[c]))

    barrier = pltpu.get_barrier_semaphore()

    others = [lax.rem(me + i, count) for i in range(1, count)]
    for device in others:
        pl.semaphore_signal(barrier, inc=1, device_id={"space": device}, device_id_type=MESH)

    load_send.wait()
    load_x.wait()
    load_tree.start()
    load_column.start()
    for load in loads:
        load.start()

    size = capacity // PIECES

    def copy_for(d, piece):
        slots = pl.ds(piece * size, size)
        return pltpu.make_async_remote_copy(
            src_ref=outgoing.at[d, slots],
            dst_ref=received.at[d, slots],
            send_sem=send_sem.at[d, piece],
            recv_sem=recv_sem.at[d, piece],
            device_id={"space": targets[d]},
            device_id_type=MESH,
        )

    for d in (2, 3, 0, 1):
        for j in range(capacity):
            outgoing[d, j] = x[send_in[d, j]]
        if d == 3:
            pl.semaphore_wait(barrier, count - 1)
            for piece in range(PIECES):
                for e in (2, 3):
                    @pl.when(sends[e])
                    def _():
                        copy_for(e, piece).start()
    for d in (0, 1):
        @pl.when(sends[d])
        def _():
            for piece in range(PIECES):
                copy_for(d, piece).start()

    load_tree.wait()
    tree = tree_in[...]
    right, right_t = doubled(tree), doubled(tree.T)

    load_column.wait()

    for load in loads:
        load.wait()

    def prepare(c, carry):
        piece = pl.ds(c * part, part)
        own = x[piece]
        extended[piece] = own
        high, low = halves(own)
        paired = jnp.concatenate([high, low], 2)
        xs[piece] = paired
        weighted = times(paired.reshape(part * nodes, 2 * species), right)
        weighted = weighted.reshape(part, nodes, species)
        z_high, z_low = halves(weighted)
        for i in range(part):
            t = c * part + i
            high, low = halves(tiles[t])
            a[t] = jnp.concatenate([high, low], 0)
        for i in range(0, part, 2):
            t = c * part + i
            turned = tiles[pl.ds(t, 2)].reshape(2 * nodes, stored * nodes).T
            high, low = halves(turned)
            both = jnp.dot(
                jnp.concatenate([high, low, high], 1),
                jnp.concatenate(
                    [apart(z_high[i], z_high[i + 1])] * 2 + [apart(z_low[i], z_low[i + 1])], 0
                ),
                preferred_element_type=jnp.float32,
            )
            for j in range(2):
                mine = both[:, j * species : (j + 1) * species]
                pull[t + j] = mine.reshape(stored, nodes, species)
        return carry

    lax.fori_loop(0, CHUNKS, prepare, 0)

    def own_entry(t, acc):
        term = pull[t, 0] * x[t]
        return acc + jnp.sum(term.reshape(nodes // 8, 8, species), axis=0)

    acc = lax.fori_loop(
        0, tile_rows, own_entry, jnp.zeros((8, species), jnp.float32), unroll=4
    )

    order = [(d, piece) for d in (0, 1) for piece in range(PIECES)]
    order += [(d, piece) for piece in range(PIECES) for d in (2, 3)]
    for d, piece in order:
        @pl.when(receives[d])
        def _():
            copy_for(d, piece).wait_recv()
            for j in range(piece * size, (piece + 1) * size):
                tile = received[d, j]
                extended[tile_rows + d * capacity + j] = tile
                high, low = halves(tile)
                xs[tile_rows + d * capacity + j] = jnp.concatenate([high, low], 1)

    def weigh(t, acc):
        for k in range(1, stored):
            term = pull[t, k] * extended[column_in[k, t]]
            acc = acc + jnp.sum(term.reshape(nodes // 8, 8, species), axis=0)
        return acc

    shares[me] = lax.fori_loop(0, tile_rows, weigh, acc, unroll=4)
    copies = [
        pltpu.make_async_remote_copy(
            src_ref=shares.at[me],
            dst_ref=shares.at[me],
            send_sem=share_send.at[i],
            recv_sem=share_recv.at[i],
            device_id={"space": device},
            device_id_type=MESH,
        )
        for i, device in enumerate(others)
    ]
    for copy in copies:
        copy.start()

    def multiply(c, carry):
        first = c * part
        piece = pl.ds(first, part)
        named = [[column_in[k, first + t] for k in range(stored)] for t in range(part)]
        product[piece] = rows_product(a.at[piece], named, xs, right_t)
        return carry

    lax.fori_loop(0, CHUNKS, multiply, 0)

    for d in range(4):
        @pl.when(sends[d])
        def _():
            for piece in range(PIECES):
                copy_for(d, piece).wait_send()
    for copy in copies:
        copy.wait_recv()
    quad_ref[0] = jnp.sum(jnp.sum(shares[...], axis=0)) * scaling
    for copy in copies:
        copy.wait_send()


def on_device(signal, space_tiles, tree_precision, send_tiles, column_tiles):
    count = lax.axis_size("space")
    tile_rows, nodes, width = space_tiles.shape
    stored = column_tiles.shape[1]
    species = signal.shape[1]
    directions, capacity = send_tiles.shape[1:]
    scaling = 1.0 / math.sqrt(count * tile_rows * nodes * species)
    vmem, f32, bf16 = pltpu.VMEM, jnp.float32, jnp.bfloat16
    dma = pltpu.SemaphoreType.DMA
    hbm = pl.BlockSpec(memory_space=pltpu.HBM)
    near = pl.BlockSpec(memory_space=vmem)
    smem = pl.BlockSpec(memory_space=pltpu.SMEM)
    field = (tile_rows, nodes, species)
    lists = (directions, capacity, nodes, species)
    columns = column_tiles.T
    flops = 2 * tile_rows * nodes * species * (width + 2 * species)
    product, quad = pl.pallas_call(
        functools.partial(kronecker_product, count, scaling),
        out_shape=(vmem(field, f32), jax.ShapeDtypeStruct((1,), f32)),
        in_specs=[hbm] * 5,
        out_specs=(near, smem),
        scratch_shapes=[
            vmem(field, f32),
            vmem(space_tiles.shape, f32),
            vmem(tree_precision.shape, f32),
            pltpu.SMEM((directions, capacity), jnp.int32),
            pltpu.SMEM(columns.shape, jnp.int32),
            vmem((tile_rows + directions * capacity, nodes, 2 * species), bf16),
            vmem((tile_rows, 2 * nodes, width), bf16),
            vmem((tile_rows + directions * capacity, nodes, species), f32),
            vmem((tile_rows, stored, nodes, species), f32),
            vmem(lists, f32),
            vmem(lists, f32),
            vmem((count, 8, species), f32),
            dma,
            dma((3,)),
            dma((CHUNKS,)),
            dma((directions, PIECES)),
            dma((directions, PIECES)),
            dma((count,)),
            dma((count,)),
        ],
        compiler_params=pltpu.CompilerParams(
            collective_id=0, has_side_effects=True, vmem_limit_bytes=40 * 2**20
        ),
        cost_estimate=pl.CostEstimate(
            flops=flops, bytes_accessed=4 * (space_tiles.size + signal.size), transcendentals=0
        ),
        name="kronecker_product",
    )(*(
        pltpu.with_memory_space_constraint(array, pltpu.HBM)
        for array in (signal.reshape(field), space_tiles, tree_precision, send_tiles[0], columns)
    ))
    return product.reshape(signal.shape), quad


def solution(mesh):
    placed = (
        P(("groups", "space"), None),
        P("space", None, None),
        P("groups", None),
        P("space", None, None),
        P("space", None),
    )
    return jax.shard_map(
        on_device,
        mesh=mesh,
        in_specs=placed,
        out_specs=(P(("groups", "space"), None), P("groups")),
        check_vma=False,
    )
```

```python
import functools
import math

import jax
import jax.numpy as jnp
from jax import lax
from jax.experimental import pallas as pl
from jax.experimental.pallas import tpu as pltpu
from jax.sharding import PartitionSpec as P

ROWS = 8
CHUNKS = 4
PIECES = 4
MESH = pl.DeviceIdType.MESH


def halves(value):
    high = value.astype(jnp.bfloat16)
    low = (value - high.astype(jnp.float32)).astype(jnp.bfloat16)
    return high, low


def doubled(matrix):
    high, low = halves(matrix)
    zero = jnp.zeros_like(low)
    return jnp.concatenate(
        [jnp.concatenate([high, low], 1), jnp.concatenate([high, zero], 1)], 0
    )


def apart(one, two):
    zero = jnp.zeros_like(one)
    return jnp.concatenate(
        [jnp.concatenate([one, zero], 1), jnp.concatenate([zero, two], 1)], 0
    )


def times(paired, weights):
    both = jnp.dot(paired, weights, preferred_element_type=jnp.float32)
    half = both.shape[1] // 2
    return both[:, :half] + both[:, half:]


def tile_product(stacked, block):
    both = jnp.dot(stacked, block, preferred_element_type=jnp.float32)
    nodes, species = both.shape[0] // 2, both.shape[1] // 2
    small = both[:nodes, species:] + both[nodes:, :species] + both[nodes:, species:]
    return both[:nodes, :species] + small


def rows_product(stacked, columns, xs, weights):
    rows = []
    for t, row_columns in enumerate(columns):
        block = jnp.concatenate([xs[c] for c in row_columns], 0)
        rows.append(tile_product(stacked[t], block))
    high, low = halves(jnp.concatenate(rows, 0))
    result = times(jnp.concatenate([high, low], 1), weights)
    return result.reshape(len(rows), -1, result.shape[-1])


def kronecker_product(
    count, scaling,
    signal_ref, tiles_ref, tree_ref, send_ref, column_ref,
    product, quad_ref,
    x, tiles, tree_in, send_in, column_in, xs, a, extended, pull, outgoing, received, inner_shares, outer_shares,
    x_sem, small_sem, tiles_sem, send_sem, recv_sem, inner_send, inner_recv, outer_send, outer_recv,
):
    tile_rows, nodes, species = x.shape
    stored = column_ref.shape[0]
    capacity = send_ref.shape[1]
    load_send = pltpu.make_async_copy(send_ref, send_in, small_sem.at[0])
    load_send.start()
    load_x = pltpu.make_async_copy(signal_ref, x, x_sem)
    load_x.start()
    load_tree = pltpu.make_async_copy(tree_ref, tree_in, small_sem.at[1])
    load_column = pltpu.make_async_copy(column_ref, column_in, small_sem.at[2])
    wide = count // ROWS
    me = lax.axis_index("space")
    column, row = lax.rem(me, wide), me // wide
    not_first, not_last = column > 0, column < wide - 1
    above, below = row > 0, row < ROWS - 1
    sends = (not_last, not_first, below, above)
    receives = (not_first, not_last, above, below)
    targets = (me + 1, me - 1, me + wide, me - wide)

    part = tile_rows // CHUNKS
    loads = []
    for c in range(CHUNKS):
        piece = pl.ds(c * part, part)
        loads.append(pltpu.make_async_copy(tiles_ref.at[piece], tiles.at[piece], tiles_sem.at[c]))

    barrier = pltpu.get_barrier_semaphore()

    def greet(device):
        pl.semaphore_signal(barrier, inc=1, device_id={"space": device}, device_id_type=MESH)

    for d in (2, 3, 0, 1):
        pl.when(sends[d])(functools.partial(greet, targets[d]))
    inner, outer = inner_shares.shape[0], outer_shares.shape[0]
    spot, team = lax.rem(me, inner), me // inner
    mates = [team * inner + lax.rem(spot + i, inner) for i in range(1, inner)]
    peers = [spot + inner * lax.rem(team + i, outer) for i in range(1, outer)]
    for device in peers + mates:
        greet(device)
    greeted = len(mates) + len(peers) + sum(jnp.where(has, 1, 0) for has in receives)

    load_send.wait()
    load_x.wait()
    load_tree.start()
    load_column.start()
    for load in loads:
        load.start()

    size = capacity // PIECES

    def copy_for(d, piece):
        slots = pl.ds(piece * size, size)
        return pltpu.make_async_remote_copy(
            src_ref=outgoing.at[d, slots],
            dst_ref=received.at[d, slots],
            send_sem=send_sem.at[d, piece],
            recv_sem=recv_sem.at[d, piece],
            device_id={"space": targets[d]},
            device_id_type=MESH,
        )

    for d in (2, 3, 0, 1):
        for j in range(capacity):
            outgoing[d, j] = x[send_in[d, j]]
        if d == 3:
            pl.semaphore_wait(barrier, greeted)
            for piece in range(PIECES):
                for e in (2, 3):
                    @pl.when(sends[e])
                    def _():
                        copy_for(e, piece).start()
    for d in (0, 1):
        @pl.when(sends[d])
        def _():
            for piece in range(PIECES):
                copy_for(d, piece).start()

    load_tree.wait()
    tree = tree_in[...]
    right, right_t = doubled(tree), doubled(tree.T)

    load_column.wait()

    for load in loads:
        load.wait()

    def prepare(c, carry):
        piece = pl.ds(c * part, part)
        own = x[piece]
        extended[piece] = own
        high, low = halves(own)
        paired = jnp.concatenate([high, low], 2)
        xs[piece] = paired
        weighted = times(paired.reshape(part * nodes, 2 * species), right)
        weighted = weighted.reshape(part, nodes, species)
        z_high, z_low = halves(weighted)
        for i in range(part):
            t = c * part + i
            high, low = halves(tiles[t])
            a[t] = jnp.concatenate([high, low], 0)
        for i in range(0, part, 2):
            t = c * part + i
            turned = tiles[pl.ds(t, 2)].reshape(2 * nodes, stored * nodes).T
            high, low = halves(turned)
            both = jnp.dot(
                jnp.concatenate([high, low, high], 1),
                jnp.concatenate(
                    [apart(z_high[i], z_high[i + 1])] * 2 + [apart(z_low[i], z_low[i + 1])], 0
                ),
                preferred_element_type=jnp.float32,
            )
            for j in range(2):
                mine = both[:, j * species : (j + 1) * species]
                pull[t + j] = mine.reshape(stored, nodes, species)
        return carry

    lax.fori_loop(0, CHUNKS, prepare, 0)

    def own_entry(t, acc):
        term = pull[t, 0] * x[t]
        return acc + jnp.sum(term.reshape(nodes // 8, 8, species), axis=0)

    acc = lax.fori_loop(
        0, tile_rows, own_entry, jnp.zeros((8, species), jnp.float32), unroll=4
    )

    order = [(d, piece) for d in (0, 1) for piece in range(PIECES)]
    order += [(d, piece) for piece in range(PIECES) for d in (2, 3)]
    for d, piece in order:
        @pl.when(receives[d])
        def _():
            copy_for(d, piece).wait_recv()
            for j in range(piece * size, (piece + 1) * size):
                tile = received[d, j]
                extended[tile_rows + d * capacity + j] = tile
                high, low = halves(tile)
                xs[tile_rows + d * capacity + j] = jnp.concatenate([high, low], 1)

    def weigh(t, acc):
        for k in range(1, stored):
            term = pull[t, k] * extended[column_in[k, t]]
            acc = acc + jnp.sum(term.reshape(nodes // 8, 8, species), axis=0)
        return acc

    inner_shares[spot] = lax.fori_loop(0, tile_rows, weigh, acc, unroll=4)
    def share_copies(shares, mine, send, receive, devices):
        return [
            pltpu.make_async_remote_copy(
                src_ref=shares.at[mine],
                dst_ref=shares.at[mine],
                send_sem=send.at[i],
                recv_sem=receive.at[i],
                device_id={"space": device},
                device_id_type=MESH,
            )
            for i, device in enumerate(devices)
        ]

    first = share_copies(inner_shares, spot, inner_send, inner_recv, mates)
    second = share_copies(outer_shares, team, outer_send, outer_recv, peers)
    for copy in first:
        copy.start()

    def multiply(c, carry):
        start = c * part
        piece = pl.ds(start, part)
        named = [[column_in[k, start + t] for k in range(stored)] for t in range(part)]
        product[piece] = rows_product(a.at[piece], named, xs, right_t)
        return carry

    lax.fori_loop(0, 1, multiply, 0)
    for copy in first:
        copy.wait_recv()
    outer_shares[team] = jnp.sum(inner_shares[...], axis=0)
    for copy in second:
        copy.start()
    lax.fori_loop(1, CHUNKS, multiply, 0)

    for d in range(4):
        @pl.when(sends[d])
        def _():
            for piece in range(PIECES):
                copy_for(d, piece).wait_send()
    for copy in second:
        copy.wait_recv()
    quad_ref[0] = jnp.sum(jnp.sum(outer_shares[...], axis=0)) * scaling
    for copy in first + second:
        copy.wait_send()


def on_device(signal, space_tiles, tree_precision, send_tiles, column_tiles):
    count = lax.axis_size("space")
    tile_rows, nodes, width = space_tiles.shape
    stored = column_tiles.shape[1]
    species = signal.shape[1]
    directions, capacity = send_tiles.shape[1:]
    inner = max(i for i in range(1, math.isqrt(count) + 1) if count % i == 0)
    scaling = 1.0 / math.sqrt(count * tile_rows * nodes * species)
    vmem, f32, bf16 = pltpu.VMEM, jnp.float32, jnp.bfloat16
    dma = pltpu.SemaphoreType.DMA
    hbm = pl.BlockSpec(memory_space=pltpu.HBM)
    near = pl.BlockSpec(memory_space=vmem)
    smem = pl.BlockSpec(memory_space=pltpu.SMEM)
    field = (tile_rows, nodes, species)
    lists = (directions, capacity, nodes, species)
    columns = column_tiles.T
    flops = 2 * tile_rows * nodes * species * (width + 2 * species)
    product, quad = pl.pallas_call(
        functools.partial(kronecker_product, count, scaling),
        out_shape=(vmem(field, f32), jax.ShapeDtypeStruct((1,), f32)),
        in_specs=[hbm] * 5,
        out_specs=(near, smem),
        scratch_shapes=[
            vmem(field, f32),
            vmem(space_tiles.shape, f32),
            vmem(tree_precision.shape, f32),
            pltpu.SMEM((directions, capacity), jnp.int32),
            pltpu.SMEM(columns.shape, jnp.int32),
            vmem((tile_rows + directions * capacity, nodes, 2 * species), bf16),
            vmem((tile_rows, 2 * nodes, width), bf16),
            vmem((tile_rows + directions * capacity, nodes, species), f32),
            vmem((tile_rows, stored, nodes, species), f32),
            vmem(lists, f32),
            vmem(lists, f32),
            vmem((inner, 8, species), f32),
            vmem((count // inner, 8, species), f32),
            dma,
            dma((3,)),
            dma((CHUNKS,)),
            dma((directions, PIECES)),
            dma((directions, PIECES)),
            dma((inner,)),
            dma((inner,)),
            dma((count // inner,)),
            dma((count // inner,)),
        ],
        compiler_params=pltpu.CompilerParams(
            collective_id=0, has_side_effects=True, vmem_limit_bytes=40 * 2**20
        ),
        cost_estimate=pl.CostEstimate(
            flops=flops, bytes_accessed=4 * (space_tiles.size + signal.size), transcendentals=0
        ),
        name="kronecker_product",
    )(*(
        pltpu.with_memory_space_constraint(array, pltpu.HBM)
        for array in (signal.reshape(field), space_tiles, tree_precision, send_tiles[0], columns)
    ))
    return product.reshape(signal.shape), quad


def solution(mesh):
    placed = (
        P(("groups", "space"), None),
        P("space", None, None),
        P("groups", None),
        P("space", None, None),
        P("space", None),
    )
    return jax.shard_map(
        on_device,
        mesh=mesh,
        in_specs=placed,
        out_specs=(P(("groups", "space"), None), P("groups")),
        check_vma=False,
    )
```

```python
import functools
import math

import jax
import jax.numpy as jnp
from jax import lax
from jax.experimental import pallas as pl
from jax.experimental.pallas import tpu as pltpu
from jax.sharding import PartitionSpec as P

ROWS = 8
CHUNKS = 4
PIECES = 4
MESH = pl.DeviceIdType.MESH


def halves(value):
    high = value.astype(jnp.bfloat16)
    low = (value - high.astype(jnp.float32)).astype(jnp.bfloat16)
    return high, low


def doubled(matrix):
    high, low = halves(matrix)
    zero = jnp.zeros_like(low)
    return jnp.concatenate(
        [jnp.concatenate([high, low], 1), jnp.concatenate([high, zero], 1)], 0
    )


def apart(one, two):
    zero = jnp.zeros_like(one)
    return jnp.concatenate(
        [jnp.concatenate([one, zero], 1), jnp.concatenate([zero, two], 1)], 0
    )


def times(paired, weights):
    both = jnp.dot(paired, weights, preferred_element_type=jnp.float32)
    half = both.shape[1] // 2
    return both[:, :half] + both[:, half:]


def tile_product(stacked, block):
    both = jnp.dot(stacked, block, preferred_element_type=jnp.float32)
    nodes, species = both.shape[0] // 2, both.shape[1] // 2
    small = both[:nodes, species:] + both[nodes:, :species] + both[nodes:, species:]
    return both[:nodes, :species] + small


def rows_product(stacked, columns, xs, weights):
    rows = []
    for t, row_columns in enumerate(columns):
        block = jnp.concatenate([xs[c] for c in row_columns], 0)
        rows.append(tile_product(stacked[t], block))
    high, low = halves(jnp.concatenate(rows, 0))
    result = times(jnp.concatenate([high, low], 1), weights)
    return result.reshape(len(rows), -1, result.shape[-1])


def kronecker_product(
    count, scaling,
    signal_ref, tiles_ref, tree_ref, send_ref, column_ref,
    product, quad_ref,
    x, tiles, tree_in, send_in, column_in, xs, a, extended, pull, outgoing, received, shares,
    x_sem, small_sem, tiles_sem, send_sem, recv_sem, share_send, share_recv,
):
    tile_rows, nodes, species = x.shape
    stored = column_ref.shape[0]
    capacity = send_ref.shape[1]
    load_send = pltpu.make_async_copy(send_ref, send_in, small_sem.at[0])
    load_send.start()
    load_x = pltpu.make_async_copy(signal_ref, x, x_sem)
    load_x.start()
    load_tree = pltpu.make_async_copy(tree_ref, tree_in, small_sem.at[1])
    load_column = pltpu.make_async_copy(column_ref, column_in, small_sem.at[2])
    wide = count // ROWS
    me = lax.axis_index("space")
    column, row = lax.rem(me, wide), me // wide
    not_first, not_last = column > 0, column < wide - 1
    above, below = row > 0, row < ROWS - 1
    sends = (not_last, not_first, below, above)
    receives = (not_first, not_last, above, below)
    targets = (me + 1, me - 1, me + wide, me - wide)

    part = tile_rows // CHUNKS
    loads = []
    for c in range(CHUNKS):
        piece = pl.ds(c * part, part)
        loads.append(pltpu.make_async_copy(tiles_ref.at[piece], tiles.at[piece], tiles_sem.at[c]))

    barrier = pltpu.get_barrier_semaphore()

    near = [wide, count - wide, 1, count - 1]
    far = [i for i in range(1, count) if i not in near]
    others = [lax.rem(me + i, count) for i in dict.fromkeys(near + far)]
    for device in others:
        pl.semaphore_signal(barrier, inc=1, device_id={"space": device}, device_id_type=MESH)

    load_send.wait()
    load_x.wait()
    load_tree.start()
    load_column.start()
    for load in loads:
        load.start()

    size = capacity // PIECES

    def copy_for(d, piece):
        slots = pl.ds(piece * size, size)
        return pltpu.make_async_remote_copy(
            src_ref=outgoing.at[d, slots],
            dst_ref=received.at[d, slots],
            send_sem=send_sem.at[d, piece],
            recv_sem=recv_sem.at[d, piece],
            device_id={"space": targets[d]},
            device_id_type=MESH,
        )

    for d in (2, 3, 0, 1):
        for j in range(capacity):
            outgoing[d, j] = x[send_in[d, j]]
        if d == 3:
            pl.semaphore_wait(barrier, count - 1)
            for piece in range(PIECES):
                for e in (2, 3):
                    @pl.when(sends[e])
                    def _():
                        copy_for(e, piece).start()
    for d in (0, 1):
        @pl.when(sends[d])
        def _():
            for piece in range(PIECES):
                copy_for(d, piece).start()

    load_tree.wait()
    tree = tree_in[...]
    right, right_t = doubled(tree), doubled(tree.T)

    load_column.wait()

    for load in loads:
        load.wait()

    def prepare(c, carry):
        piece = pl.ds(c * part, part)
        own = x[piece]
        extended[piece] = own
        high, low = halves(own)
        paired = jnp.concatenate([high, low], 2)
        xs[piece] = paired
        weighted = times(paired.reshape(part * nodes, 2 * species), right)
        weighted = weighted.reshape(part, nodes, species)
        z_high, z_low = halves(weighted)
        for i in range(part):
            t = c * part + i
            high, low = halves(tiles[t])
            a[t] = jnp.concatenate([high, low], 0)
        for i in range(0, part, 2):
            t = c * part + i
            turned = tiles[pl.ds(t, 2)].reshape(2 * nodes, stored * nodes).T
            high, low = halves(turned)
            both = jnp.dot(
                jnp.concatenate([high, low, high], 1),
                jnp.concatenate(
                    [apart(z_high[i], z_high[i + 1])] * 2 + [apart(z_low[i], z_low[i + 1])], 0
                ),
                preferred_element_type=jnp.float32,
            )
            for j in range(2):
                mine = both[:, j * species : (j + 1) * species]
                pull[t + j] = mine.reshape(stored, nodes, species)
        return carry

    lax.fori_loop(0, CHUNKS, prepare, 0)

    def own_entry(t, acc):
        term = pull[t, 0] * x[t]
        return acc + jnp.sum(term.reshape(nodes // 8, 8, species), axis=0)

    acc = lax.fori_loop(
        0, tile_rows, own_entry, jnp.zeros((8, species), jnp.float32), unroll=4
    )

    order = [(d, piece) for d in (0, 1) for piece in range(PIECES)]
    order += [(d, piece) for piece in range(PIECES) for d in (2, 3)]
    for d, piece in order:
        @pl.when(receives[d])
        def _():
            copy_for(d, piece).wait_recv()
            for j in range(piece * size, (piece + 1) * size):
                tile = received[d, j]
                extended[tile_rows + d * capacity + j] = tile
                high, low = halves(tile)
                xs[tile_rows + d * capacity + j] = jnp.concatenate([high, low], 1)

    def weigh(t, acc):
        for k in range(1, stored):
            term = pull[t, k] * extended[column_in[k, t]]
            acc = acc + jnp.sum(term.reshape(nodes // 8, 8, species), axis=0)
        return acc

    shares[me] = lax.fori_loop(0, tile_rows, weigh, acc, unroll=4)
    copies = [
        pltpu.make_async_remote_copy(
            src_ref=shares.at[me],
            dst_ref=shares.at[me],
            send_sem=share_send.at[i],
            recv_sem=share_recv.at[i],
            device_id={"space": device},
            device_id_type=MESH,
        )
        for i, device in enumerate(others)
    ]
    for copy in copies:
        copy.start()

    def multiply(c, carry):
        first = c * part
        piece = pl.ds(first, part)
        named = [[column_in[k, first + t] for k in range(stored)] for t in range(part)]
        product[piece] = rows_product(a.at[piece], named, xs, right_t)
        return carry

    lax.fori_loop(0, CHUNKS, multiply, 0)

    for d in range(4):
        @pl.when(sends[d])
        def _():
            for piece in range(PIECES):
                copy_for(d, piece).wait_send()
    for copy in copies:
        copy.wait_recv()
    total = jnp.sum(shares[...], axis=0)
    quad_ref[...] = jnp.sum(total, axis=(0, 1), keepdims=True) * scaling
    for copy in copies:
        copy.wait_send()


def on_device(signal, space_tiles, tree_precision, send_tiles, column_tiles):
    count = lax.axis_size("space")
    tile_rows, nodes, width = space_tiles.shape
    stored = column_tiles.shape[1]
    species = signal.shape[1]
    directions, capacity = send_tiles.shape[1:]
    scaling = 1.0 / math.sqrt(count * tile_rows * nodes * species)
    vmem, f32, bf16 = pltpu.VMEM, jnp.float32, jnp.bfloat16
    dma = pltpu.SemaphoreType.DMA
    hbm = pl.BlockSpec(memory_space=pltpu.HBM)
    near = pl.BlockSpec(memory_space=vmem)
    field = (tile_rows, nodes, species)
    lists = (directions, capacity, nodes, species)
    columns = column_tiles.T
    flops = 2 * tile_rows * nodes * species * (width + 2 * species)
    product, quad = pl.pallas_call(
        functools.partial(kronecker_product, count, scaling),
        out_shape=(vmem(field, f32), vmem((1, 1), f32)),
        in_specs=[hbm] * 5,
        out_specs=(near, near),
        scratch_shapes=[
            vmem(field, f32),
            vmem(space_tiles.shape, f32),
            vmem(tree_precision.shape, f32),
            pltpu.SMEM((directions, capacity), jnp.int32),
            pltpu.SMEM(columns.shape, jnp.int32),
            vmem((tile_rows + directions * capacity, nodes, 2 * species), bf16),
            vmem((tile_rows, 2 * nodes, width), bf16),
            vmem((tile_rows + directions * capacity, nodes, species), f32),
            vmem((tile_rows, stored, nodes, species), f32),
            vmem(lists, f32),
            vmem(lists, f32),
            vmem((count, 8, species), f32),
            dma,
            dma((3,)),
            dma((CHUNKS,)),
            dma((directions, PIECES)),
            dma((directions, PIECES)),
            dma((count,)),
            dma((count,)),
        ],
        compiler_params=pltpu.CompilerParams(
            collective_id=0, has_side_effects=True, vmem_limit_bytes=40 * 2**20
        ),
        cost_estimate=pl.CostEstimate(
            flops=flops, bytes_accessed=4 * (space_tiles.size + signal.size), transcendentals=0
        ),
        name="kronecker_product",
    )(*(
        pltpu.with_memory_space_constraint(array, pltpu.HBM)
        for array in (signal.reshape(field), space_tiles, tree_precision, send_tiles[0], columns)
    ))
    return product.reshape(signal.shape), quad.reshape(1)


def solution(mesh):
    placed = (
        P(("groups", "space"), None),
        P("space", None, None),
        P("groups", None),
        P("space", None, None),
        P("space", None),
    )
    return jax.shard_map(
        on_device,
        mesh=mesh,
        in_specs=placed,
        out_specs=(P(("groups", "space"), None), P("groups")),
        check_vma=False,
    )
```

```python
import functools
import math

import jax
import jax.numpy as jnp
from jax import lax
from jax.experimental import pallas as pl
from jax.experimental.pallas import tpu as pltpu
from jax.sharding import PartitionSpec as P

ROWS = 8
CHUNKS = 4
PIECES = 4
MESH = pl.DeviceIdType.MESH


def halves(value):
    high = value.astype(jnp.bfloat16)
    low = (value - high.astype(jnp.float32)).astype(jnp.bfloat16)
    return high, low


def doubled(matrix):
    high, low = halves(matrix)
    zero = jnp.zeros_like(low)
    return jnp.concatenate(
        [jnp.concatenate([high, low], 1), jnp.concatenate([high, zero], 1)], 0
    )


def apart(one, two):
    zero = jnp.zeros_like(one)
    return jnp.concatenate(
        [jnp.concatenate([one, zero], 1), jnp.concatenate([zero, two], 1)], 0
    )


def times(paired, weights):
    both = jnp.dot(paired, weights, preferred_element_type=jnp.float32)
    half = both.shape[1] // 2
    return both[:, :half] + both[:, half:]


def tile_product(stacked, block):
    both = jnp.dot(stacked, block, preferred_element_type=jnp.float32)
    nodes, species = both.shape[0] // 2, both.shape[1] // 2
    small = both[:nodes, species:] + both[nodes:, :species] + both[nodes:, species:]
    return both[:nodes, :species] + small


def rows_product(stacked, columns, xs, weights):
    rows = []
    for t, row_columns in enumerate(columns):
        block = jnp.concatenate([xs[c] for c in row_columns], 0)
        rows.append(tile_product(stacked[t], block))
    high, low = halves(jnp.concatenate(rows, 0))
    result = times(jnp.concatenate([high, low], 1), weights)
    return result.reshape(len(rows), -1, result.shape[-1])


def kronecker_product(
    count, scaling,
    signal_ref, tiles_ref, tree_ref, send_ref, column_ref,
    product, quad_ref,
    x, tiles, tree_in, send_in, column_in, xs, a, extended, pull, outgoing, received, shares,
    x_sem, small_sem, tiles_sem, send_sem, recv_sem, share_send, share_recv,
):
    tile_rows, nodes, species = x.shape
    stored = column_ref.shape[0]
    capacity = send_ref.shape[1]
    load_send = pltpu.make_async_copy(send_ref, send_in, small_sem.at[0])
    load_send.start()
    load_x = pltpu.make_async_copy(signal_ref, x, x_sem)
    load_x.start()
    load_tree = pltpu.make_async_copy(tree_ref, tree_in, small_sem.at[1])
    load_column = pltpu.make_async_copy(column_ref, column_in, small_sem.at[2])
    wide = count // ROWS
    me = lax.axis_index("space")
    column, row = lax.rem(me, wide), me // wide
    not_first, not_last = column > 0, column < wide - 1
    above, below = row > 0, row < ROWS - 1
    sends = (not_last, not_first, below, above)
    receives = (not_first, not_last, above, below)
    targets = (me + 1, me - 1, me + wide, me - wide)

    part = tile_rows // CHUNKS
    loads = []
    for c in range(CHUNKS):
        piece = pl.ds(c * part, part)
        loads.append(pltpu.make_async_copy(tiles_ref.at[piece], tiles.at[piece], tiles_sem.at[c]))

    barrier = pltpu.get_barrier_semaphore()

    near = [wide, count - wide, 1, count - 1]
    far = [i for i in range(1, count) if i not in near]
    others = [lax.rem(me + i, count) for i in dict.fromkeys(near + far)]
    for device in others:
        pl.semaphore_signal(barrier, inc=1, device_id={"space": device}, device_id_type=MESH)

    load_send.wait()
    load_x.wait()
    load_tree.start()
    load_column.start()
    for load in loads:
        load.start()

    size = capacity // PIECES

    def copy_for(d, piece):
        slots = pl.ds(piece * size, size)
        return pltpu.make_async_remote_copy(
            src_ref=outgoing.at[d, slots],
            dst_ref=received.at[d, slots],
            send_sem=send_sem.at[d, piece],
            recv_sem=recv_sem.at[d, piece],
            device_id={"space": targets[d]},
            device_id_type=MESH,
        )

    for d in (2, 3, 0, 1):
        for j in range(capacity):
            outgoing[d, j] = x[send_in[d, j]]
        if d == 3:
            pl.semaphore_wait(barrier, count - 1)
            for piece in range(PIECES):
                for e in (2, 3):
                    @pl.when(sends[e])
                    def _():
                        copy_for(e, piece).start()
    for d in (0, 1):
        @pl.when(sends[d])
        def _():
            for piece in range(PIECES):
                copy_for(d, piece).start()

    load_tree.wait()
    tree = tree_in[...]
    right, right_t = doubled(tree), doubled(tree.T)

    load_column.wait()

    for load in loads:
        load.wait()

    def prepare(c, carry):
        piece = pl.ds(c * part, part)
        own = x[piece]
        extended[piece] = own
        high, low = halves(own)
        paired = jnp.concatenate([high, low], 2)
        xs[piece] = paired
        weighted = times(paired.reshape(part * nodes, 2 * species), right)
        weighted = weighted.reshape(part, nodes, species)
        z_high, z_low = halves(weighted)
        for i in range(part):
            t = c * part + i
            high, low = halves(tiles[t])
            a[t] = jnp.concatenate([high, low], 0)
        for i in range(0, part, 2):
            t = c * part + i
            turned = tiles[pl.ds(t, 2)].reshape(2 * nodes, stored * nodes).T
            high, low = halves(turned)
            both = jnp.dot(
                jnp.concatenate([high, low, high], 1),
                jnp.concatenate(
                    [apart(z_high[i], z_high[i + 1])] * 2 + [apart(z_low[i], z_low[i + 1])], 0
                ),
                preferred_element_type=jnp.float32,
            )
            for j in range(2):
                mine = both[:, j * species : (j + 1) * species]
                pull[t + j] = mine.reshape(stored, nodes, species)
        return carry

    lax.fori_loop(0, CHUNKS, prepare, 0)

    def own_entry(t, acc):
        term = pull[t, 0] * x[t]
        return acc + jnp.sum(term.reshape(nodes // 8, 8, species), axis=0)

    acc = lax.fori_loop(
        0, tile_rows, own_entry, jnp.zeros((8, species), jnp.float32), unroll=4
    )

    order = [(d, piece) for d in (0, 1) for piece in range(PIECES)]
    order += [(d, piece) for piece in range(PIECES) for d in (2, 3)]
    for d, piece in order:
        @pl.when(receives[d])
        def _():
            copy_for(d, piece).wait_recv()
            for j in range(piece * size, (piece + 1) * size):
                tile = received[d, j]
                extended[tile_rows + d * capacity + j] = tile
                high, low = halves(tile)
                xs[tile_rows + d * capacity + j] = jnp.concatenate([high, low], 1)

    def weigh(t, acc):
        for k in range(1, stored):
            term = pull[t, k] * extended[column_in[k, t]]
            acc = acc + jnp.sum(term.reshape(nodes // 8, 8, species), axis=0)
        return acc

    shares[me] = lax.fori_loop(0, tile_rows, weigh, acc, unroll=4)
    copies = [
        pltpu.make_async_remote_copy(
            src_ref=shares.at[me],
            dst_ref=shares.at[me],
            send_sem=share_send.at[i],
            recv_sem=share_recv.at[i],
            device_id={"space": device},
            device_id_type=MESH,
        )
        for i, device in enumerate(others)
    ]
    for copy in reversed(copies):
        copy.start()

    def multiply(c, carry):
        first = c * part
        piece = pl.ds(first, part)
        named = [[column_in[k, first + t] for k in range(stored)] for t in range(part)]
        product[piece] = rows_product(a.at[piece], named, xs, right_t)
        return carry

    lax.fori_loop(0, CHUNKS, multiply, 0)

    for d in range(4):
        @pl.when(sends[d])
        def _():
            for piece in range(PIECES):
                copy_for(d, piece).wait_send()
    for copy in copies:
        copy.wait_recv()
    total = jnp.sum(shares[...], axis=0)
    quad_ref[...] = jnp.sum(total, axis=(0, 1), keepdims=True) * scaling
    for copy in copies:
        copy.wait_send()


def on_device(signal, space_tiles, tree_precision, send_tiles, column_tiles):
    count = lax.axis_size("space")
    tile_rows, nodes, width = space_tiles.shape
    stored = column_tiles.shape[1]
    species = signal.shape[1]
    directions, capacity = send_tiles.shape[1:]
    scaling = 1.0 / math.sqrt(count * tile_rows * nodes * species)
    vmem, f32, bf16 = pltpu.VMEM, jnp.float32, jnp.bfloat16
    dma = pltpu.SemaphoreType.DMA
    hbm = pl.BlockSpec(memory_space=pltpu.HBM)
    near = pl.BlockSpec(memory_space=vmem)
    field = (tile_rows, nodes, species)
    lists = (directions, capacity, nodes, species)
    columns = column_tiles.T
    flops = 2 * tile_rows * nodes * species * (width + 2 * species)
    product, quad = pl.pallas_call(
        functools.partial(kronecker_product, count, scaling),
        out_shape=(vmem(field, f32), vmem((1, 1), f32)),
        in_specs=[hbm] * 5,
        out_specs=(near, near),
        scratch_shapes=[
            vmem(field, f32),
            vmem(space_tiles.shape, f32),
            vmem(tree_precision.shape, f32),
            pltpu.SMEM((directions, capacity), jnp.int32),
            pltpu.SMEM(columns.shape, jnp.int32),
            vmem((tile_rows + directions * capacity, nodes, 2 * species), bf16),
            vmem((tile_rows, 2 * nodes, width), bf16),
            vmem((tile_rows + directions * capacity, nodes, species), f32),
            vmem((tile_rows, stored, nodes, species), f32),
            vmem(lists, f32),
            vmem(lists, f32),
            vmem((count, 8, species), f32),
            dma,
            dma((3,)),
            dma((CHUNKS,)),
            dma((directions, PIECES)),
            dma((directions, PIECES)),
            dma((count,)),
            dma((count,)),
        ],
        compiler_params=pltpu.CompilerParams(
            collective_id=0, has_side_effects=True, vmem_limit_bytes=40 * 2**20
        ),
        cost_estimate=pl.CostEstimate(
            flops=flops, bytes_accessed=4 * (space_tiles.size + signal.size), transcendentals=0
        ),
        name="kronecker_product",
    )(*(
        pltpu.with_memory_space_constraint(array, pltpu.HBM)
        for array in (signal.reshape(field), space_tiles, tree_precision, send_tiles[0], columns)
    ))
    return product.reshape(signal.shape), quad.reshape(1)


def solution(mesh):
    placed = (
        P(("groups", "space"), None),
        P("space", None, None),
        P("groups", None),
        P("space", None, None),
        P("space", None),
    )
    return jax.shard_map(
        on_device,
        mesh=mesh,
        in_specs=placed,
        out_specs=(P(("groups", "space"), None), P("groups")),
        check_vma=False,
    )
```
